32 devices in a mesh: tm: 4 (over y, core), space: 4 (over z), dp: 2 (over x).
Axes of the slice: x: 2, y: 2, z: 4, core: 2. Of those that a mesh axis runs over, the one named last changes fastest.
Arguments:
- latents: bfloat16 [2, 1024, 2048], P('dp', 'tm'), may hold values from -6 to 6
- proj_input: bfloat16 [2048, 128], replicated, may hold values from -0.125 to 0.125
- proj_output: bfloat16 [2048, 128], replicated, may hold values from -0.125 to 0.125
- scan_input: bfloat16 [2, 1024, 4096], P('dp', 'tm', 'space'), may hold values from -6 to 6
- log_decay: float32 [2, 1024, 32], P('dp', 'tm', 'space'), may hold values from -2 to 0
- att_queries: bfloat16 [2, 1024, 4096], P('dp', 'tm', 'space'), may hold values from -67.88225 to 67.88225
- att_keys: bfloat16 [2, 1024, 4096], P('dp', 'tm', 'space'), may hold values from -3 to 3
- att_values: bfloat16 [2, 1024, 4096], P('dp', 'tm', 'space'), may hold values from -6 to 6
- scan_cotangent: bfloat16 [2, 1024, 4096], P('dp', 'tm', 'space'), may hold values from -0.59765625 to 0.59765625
- window_offsets: int32 [2, 8], P('dp', 'tm'), may hold values from 0 to 63
Outputs:
- layer_out: bfloat16 [2, 1024, 4096], P('dp', 'tm', 'space')
- input_grad: bfloat16 [2, 1024, 4096], P('dp', 'tm', 'space')
- proj_grad: float32 [2048, 256], P('space')
The draws below stay inside these ranges and needn't reach their ends.
All inputs are finite; a program needn't handle non-finite values.
Results may differ from the reference program's by a relative error of at most 0.027.
Values may be sent and summed in bfloat16 or wider, within the bound.
A program may use at most 64 MiB of HBM per device.

```python
import math
import jax
import jax.numpy as jnp
from jax import lax

D = 2048
N = 128
H = 32
P_SIZE = 128
W = 128
QB = 128
TOK_DEV = 256
SEQ = 1024
CLIPS = 2


def key_base(key):
    return jnp.clip(jax.random.normal(jax.random.fold_in(key, 11), (CLIPS, SEQ, H * P_SIZE), jnp.float32), -3.0, 3.0)


def draw_att_keys(key, part):
    base = key_base(key)
    return base.astype(jnp.bfloat16)


def draw_att_queries(key, part):
    query = jnp.clip(jax.random.normal(jax.random.fold_in(key, 12), (CLIPS, SEQ, H * P_SIZE), jnp.float32), -3.0, 3.0)
    return query.astype(jnp.bfloat16)


def draw_log_decay(key, part):
    parts_of_key = jax.random.split(jax.random.fold_in(key, 13), 7)
    slow = -jax.random.uniform(parts_of_key[0], (CLIPS, 1, H), jnp.float32, 0.2, 0.6) / SEQ
    fast = -1.0 / jax.random.uniform(parts_of_key[1], (CLIPS, 1, H), jnp.float32, 30.0, 50.0)
    fast_share = 0.5
    picked = jax.random.uniform(parts_of_key[2], (CLIPS, 1, H), jnp.float32) < fast_share
    base = jnp.where(picked, fast, slow)
    rough = jnp.exp(jax.random.uniform(parts_of_key[3], (CLIPS, SEQ, H), jnp.float32, -0.69, 0.69))
    blocky = jnp.exp(jax.random.uniform(parts_of_key[4], (CLIPS, SEQ // TOK_DEV, 1, H), jnp.float32, -0.69, 0.69))
    blocky = jnp.broadcast_to(blocky, (CLIPS, SEQ // TOK_DEV, TOK_DEV, H)).reshape(CLIPS, SEQ, H)
    decay_speeds = base * rough * blocky
    spots = jax.random.randint(parts_of_key[5], (CLIPS, 2, 1), 0, SEQ)
    loss_values = jnp.log(jax.random.uniform(parts_of_key[6], (CLIPS, 2, H), jnp.float32, 0.5, 0.8))
    token_places = jnp.arange(SEQ)
    hit_mask = (token_places[None, None, :] == spots).astype(jnp.float32)
    spike_train = jnp.sum(hit_mask[:, :, :, None] * loss_values[:, :, None, :], axis=1)
    return decay_speeds + spike_train


def touch_ends(entries, own_key, least, largest):
    index_at = [jax.random.randint(jax.random.fold_in(own_key, axis), (), 0, length) for axis, length in enumerate(entries.shape)]
    longest = entries.shape.index(max(entries.shape))
    next_to = index_at[:longest] + [(index_at[longest] + 1) % entries.shape[longest]] + index_at[longest + 1:]
    return entries.at[tuple(index_at)].set(least).at[tuple(next_to)].set(largest)


def spiked(values, stream_key, source, target, parts, factor):
    def block_of(axis_at):
        return (jnp.arange(values.shape[axis_at]) // (values.shape[axis_at] // parts)).reshape((-1,) + (1,) * (values.ndim - 1 - axis_at))

    first = jax.random.permutation(stream_key, parts)[block_of(target)]
    far = (block_of(target) + parts // 2) % parts
    return jnp.where((block_of(source) == first) | (block_of(source) == far), factor * values, values)


def block_scale(own_key, shape, pieces, low, high):
    factor_of = 1.0
    for dim, shards_of in pieces:
        draws = jax.random.uniform(jax.random.fold_in(jax.random.fold_in(own_key, 6), dim), (shards_of,), jnp.float32, low / len(pieces), high / len(pieces))
        factor_of = factor_of * jnp.repeat(jnp.exp(draws), shape[dim] // shards_of).reshape((-1,) + (1,) * (len(shape) - 1 - dim))
    return factor_of


def scatter_about(key, extent, scale, limit, pieces=(), kind=jnp.bfloat16):
    values = scale * jax.random.normal(key, extent, jnp.float32)
    if pieces:
        values = values * block_scale(key, extent, pieces, -0.22, 0.18)
    return jnp.clip(values, -limit, limit).astype(kind)


def heavy_noise(stream_key, dims, spread, limit, pieces, heavy, held_as=jnp.bfloat16):
    entries = spread * jax.random.normal(stream_key, dims, jnp.float32)
    if pieces:
        entries = entries * block_scale(stream_key, dims, pieces, -0.22, 0.18)
    return jnp.clip(spiked(entries, jax.random.fold_in(stream_key, 3), *heavy), -limit, limit).astype(held_as)


def setup_inputs(seed: int = 0) -> dict:
    key_of = jax.random.split(jax.random.key(seed), 11)
    return {
        "latents": heavy_noise(key_of[0], (CLIPS, SEQ, D), 1.0, 6.0, ((0, 2), (1, 4)), (1, 2, 4, 2.0)),
        "proj_input": scatter_about(key_of[1], (D, N), D ** -0.5, 0.125),
        "proj_output": scatter_about(key_of[2], (D, N), D ** -0.5, 0.125),
        "scan_input": scatter_about(key_of[3], (CLIPS, SEQ, H * P_SIZE), 1.0, 6.0, ((0, 2), (1, 4), (2, 4))),
        "log_decay": draw_log_decay(jax.random.fold_in(key_of[10], 71), 0),
        "att_queries": draw_att_queries(jax.random.fold_in(key_of[10], 71), 0),
        "att_keys": draw_att_keys(jax.random.fold_in(key_of[10], 71), 0),
        "att_values": scatter_about(key_of[7], (CLIPS, SEQ, H * P_SIZE), 1.0, 6.0, ((0, 2), (1, 4), (2, 4))),
        "scan_cotangent": scatter_about(key_of[8], (CLIPS, SEQ, H * P_SIZE), 0.1, 0.59765625, ((0, 2), (1, 4), (2, 4))),
        "window_offsets": touch_ends(jax.random.randint(key_of[9], (CLIPS, SEQ // QB), 0, W // 2), jax.random.fold_in(key_of[9], 1), 0, (W // 2) - 1).astype(jnp.int32),
    }


precise = lax.Precision.HIGHEST

def block_decay(cum_decay):
    row_count = cum_decay.shape[0]
    position = jnp.arange(row_count, dtype=jnp.int32)
    lower_mask = position[:, None] >= position[None, :]
    log_gap = cum_decay.T[:, :, None] - cum_decay.T[:, None, :]
    return jnp.exp(jnp.where(lower_mask[None], log_gap, -jnp.inf))

def reference(latents, proj_input, proj_output, scan_input, log_decay, att_queries, att_keys, att_values, scan_cotangent, window_offsets):
    state_scale = 1.0 / math.sqrt(N)
    block_count = SEQ // TOK_DEV
    row_count = TOK_DEV

    def one_clip(data):
        lat_rows, scan_rows, decay_rows, query_rows, key_rows, value_rows, cotan_rows, offset_rows = data
        b_rows = jnp.dot(lat_rows, proj_input, preferred_element_type=jnp.float32).astype(jnp.bfloat16)
        c_rows = jnp.dot(lat_rows, proj_output, preferred_element_type=jnp.float32).astype(jnp.bfloat16)
        cum_decay = jnp.cumsum(decay_rows.astype(jnp.float32).reshape(block_count, row_count, H), axis=1)
        scan_blocks = scan_rows.reshape(block_count, row_count, H, P_SIZE)
        cotan_blocks = cotan_rows.reshape(block_count, row_count, H, P_SIZE)
        b_blocks = b_rows.reshape(block_count, row_count, N)
        c_blocks = c_rows.reshape(block_count, row_count, N)
        lat_blocks = lat_rows.reshape(block_count, row_count, D)

        def mixing_of(b_blk, c_blk, cum_blk):
            decay_mat = block_decay(cum_blk)
            kernel = jnp.dot(c_blk, b_blk.T, preferred_element_type=jnp.float32) * state_scale
            return (decay_mat, (kernel[None] * decay_mat).astype(jnp.bfloat16))

        def forward(state, item):
            scan_blk, b_blk, c_blk, cum_blk = item
            decay_mat, mixing = mixing_of(b_blk, c_blk, cum_blk)
            inner = jnp.einsum('hts,shp->thp', mixing.astype(jnp.float32), scan_blk.astype(jnp.float32))
            block_total = cum_blk[-1]
            cross = jnp.exp(cum_blk)[:, :, None] * jnp.einsum('tn,hpn->thp', c_blk.astype(jnp.float32) * state_scale, state, precision=precise)
            weighted = scan_blk.astype(jnp.float32) * jnp.exp(block_total[None] - cum_blk)[:, :, None]
            fresh = jnp.einsum('shp,sn->hpn', weighted, b_blk.astype(jnp.float32), precision=precise)
            new_state = jnp.exp(block_total)[:, None, None] * state + fresh
            return (new_state, (inner + cross, state))
        zero_state = jnp.zeros((H, P_SIZE, N), jnp.float32)
        _, (scan_out, state_in) = lax.scan(forward, zero_state, (scan_blocks, b_blocks, c_blocks, cum_decay))
        normed = scan_out * lax.rsqrt(lax.optimization_barrier(jnp.mean(scan_out * scan_out, axis=-1, keepdims=True)) + 1e-05)
        key_pad = jnp.concatenate([jnp.zeros((W, H * P_SIZE), key_rows.dtype), key_rows], 0)
        value_pad = jnp.concatenate([jnp.zeros((W, H * P_SIZE), value_rows.dtype), value_rows], 0)

        def attend(block):
            start = block * row_count
            query_blk = lax.dynamic_slice_in_dim(query_rows, start, row_count, 0).reshape(row_count, H, P_SIZE)
            key_blk = lax.dynamic_slice_in_dim(key_pad, start, row_count + W, 0).reshape(row_count + W, H, P_SIZE)
            value_blk = lax.dynamic_slice_in_dim(value_pad, start, row_count + W, 0).reshape(row_count + W, H, P_SIZE)
            offset_blk = lax.dynamic_slice_in_dim(offset_rows, block * (row_count // QB), row_count // QB, 0)
            offset_each = jnp.repeat(offset_blk, QB)
            t_pos = start + jnp.arange(row_count, dtype=jnp.int32)
            s_pos = start - W + jnp.arange(row_count + W, dtype=jnp.int32)
            seen = (s_pos[None] <= t_pos[:, None]) & (s_pos[None] >= t_pos[:, None] - W + 1 + offset_each[:, None]) & (s_pos[None] >= 0)
            scores = jnp.einsum('thp,shp->hts', query_blk.astype(jnp.float32), key_blk.astype(jnp.float32)) / math.sqrt(P_SIZE)
            scores = jnp.where(seen[None], scores, -jnp.inf)
            highest = lax.optimization_barrier(jnp.max(scores, axis=-1, keepdims=True))
            expo = jnp.exp(scores - highest)
            probs = (expo / lax.optimization_barrier(jnp.sum(expo, axis=-1, keepdims=True))).astype(jnp.bfloat16)
            return jnp.einsum('hts,shp->thp', probs.astype(jnp.float32), value_blk.astype(jnp.float32))
        attended = lax.map(attend, jnp.arange(block_count, dtype=jnp.int32))
        layer_out = (normed + attended).reshape(SEQ, H * P_SIZE).astype(jnp.bfloat16)

        def backward(carry, item):
            back_state, grad_sum = carry
            scan_blk, cotan_blk, b_blk, c_blk, cum_blk, enter_blk, lat_blk = item
            decay_mat, mixing = mixing_of(b_blk, c_blk, cum_blk)
            block_total = cum_blk[-1]
            tail_fall = jnp.exp(block_total[None] - cum_blk)
            head_rise = jnp.exp(cum_blk)
            scan_f = scan_blk.astype(jnp.float32)
            cotan_f = cotan_blk.astype(jnp.float32)
            b_f = b_blk.astype(jnp.float32)
            c_f = c_blk.astype(jnp.float32)
            grad_x = jnp.einsum('hts,thp->shp', mixing.astype(jnp.float32), cotan_f)
            grad_x = grad_x + tail_fall[:, :, None] * jnp.einsum('hpn,sn->shp', back_state, b_f, precision=precise)
            product = jnp.einsum('thp,shp->hts', cotan_f, scan_f)
            weigh = (product * decay_mat * state_scale).astype(jnp.bfloat16).astype(jnp.float32)
            grad_b = jnp.einsum('hts,tn->hsn', weigh, c_f) + tail_fall.T[:, :, None] * jnp.einsum('shp,hpn->hsn', scan_f, back_state, precision=precise)
            gradient_readout = jnp.einsum('hts,sn->htn', weigh, b_f) + (head_rise.T * state_scale)[:, :, None] * jnp.einsum('thp,hpn->htn', cotan_f, enter_blk, precision=precise)
            both = jnp.concatenate([grad_b, gradient_readout], axis=-1).astype(jnp.bfloat16).astype(jnp.float32)
            head_summed = lax.optimization_barrier(jnp.sum(both, axis=0))
            grad_sum = grad_sum + jnp.dot(lat_blk.astype(jnp.float32).T, head_summed, precision=precise)
            fresh = jnp.einsum('thp,tn->hpn', cotan_f * head_rise[:, :, None], c_f * state_scale, precision=precise)
            back_state = jnp.exp(block_total)[:, None, None] * back_state + fresh
            return ((back_state, grad_sum), grad_x)
        start_carry = (zero_state, jnp.zeros((D, 2 * N), jnp.float32))
        items = (scan_blocks, cotan_blocks, b_blocks, c_blocks, cum_decay, state_in, lat_blocks)
        (_, grad_sum), grad_x = lax.scan(backward, start_carry, items, reverse=True)
        return (layer_out, grad_x.reshape(SEQ, H * P_SIZE).astype(jnp.bfloat16), grad_sum)
    layer_out, input_grad, grad_parts = lax.map(one_clip, (latents, scan_input, log_decay, att_queries, att_keys, att_values, scan_cotangent, window_offsets))
    proj_grad = lax.optimization_barrier(jnp.sum(grad_parts, axis=0)) / math.sqrt(CLIPS * SEQ)
    return (layer_out, input_grad, proj_grad)
```

```python
import functools
import math

import jax
import jax.numpy as jnp
from jax import lax
from jax.experimental import pallas as pl
from jax.experimental.pallas import tpu as pltpu
from jax.sharding import PartitionSpec as P

W = 128
QB = 128
MESH = pl.DeviceIdType.MESH
BF = jnp.bfloat16
F32 = jnp.float32
HI = lax.Precision.HIGHEST


def mm(a, b, ca=1, cb=0, precision=None):
    return lax.dot_general(
        a, b, (((ca,), (cb,)), ((), ())), preferred_element_type=F32, precision=precision
    )


def kernel(
    sizes,
    lat_h, pi_h, po_h, x_h, ld_ref, q_h, k_h, v_h, g_h, off_ref,
    lo_h, ig_h, pg_h,
    lat, pi, po, x, g, q, kx, vx, lo, ig, pg,
    cumb, cumt, b_s, c_s, cs_s, kern, wsum, xw, rg, inner, gx, att,
    f_fresh, f_in, f_out, r_fresh, r_in, r_out,
    both, rz, zfull, term, rs, agf,
    load_sem, store_sem, chain_send, chain_recv, halo_send, halo_recv,
    zs_send, zs_recv, zg_send, zg_recv, rs_send, rs_recv, ag_send, ag_recv,
):
    n_tm, n_z, n_dp = sizes
    rows, width = x.shape
    heads = ld_ref.shape[1]
    dim = width // heads
    states = pi.shape[1]
    scale = 1.0 / math.sqrt(states)
    group = n_tm * n_dp
    share = lat.shape[1] // n_z
    owners = min(group, share // 16)
    chunk = share // owners
    zrows = rows // n_z
    tm = lax.axis_index("tm")
    z = lax.axis_index("space")
    dp = lax.axis_index("dp")
    me = dp * n_tm + tm

    def member(k):
        other = lax.rem(me + k, group)
        return other, {"dp": other // n_tm, "tm": lax.rem(other, n_tm)}

    def zmember(k):
        other = lax.rem(z + k, n_z)
        return other, {"space": other}

    loads = [
        pltpu.make_async_copy(src, dst, load_sem.at[i])
        for i, (src, dst) in enumerate(
            [
                (lat_h, lat), (pi_h, pi), (po_h, po), (x_h, x), (g_h, g),
                (k_h, kx.at[pl.ds(W, rows)]), (v_h, vx.at[pl.ds(W, rows)]), (q_h, q),
            ]
        )
    ]
    for load in loads:
        load.start()

    barrier = pltpu.get_barrier_semaphore()
    for k in range(1, group):
        pl.semaphore_signal(barrier, inc=1, device_id=member(k)[1], device_id_type=MESH)
    for k in range(1, n_z):
        pl.semaphore_signal(barrier, inc=1, device_id=zmember(k)[1], device_id_type=MESH)

    row_i = lax.broadcasted_iota(jnp.int32, (rows, rows), 0)
    col_i = lax.broadcasted_iota(jnp.int32, (rows, rows), 1)
    lower = (row_i >= col_i).astype(F32)
    ld = ld_ref[...]
    cum = mm(lower, ld, precision=HI)
    cumt[...] = mm(ld, lower, 0, 1, precision=HI)
    spread = (
        lax.broadcasted_iota(jnp.int32, (heads, width), 1) // dim
        == lax.broadcasted_iota(jnp.int32, (heads, width), 0)
    ).astype(F32)
    cumb[...] = mm(cum, spread, precision=HI)

    for load in loads[:3]:
        load.wait()
    b_s[...] = mm(lat[...], pi[...]).astype(BF)
    cf = mm(lat[...], po[...]).astype(BF)
    c_s[...] = cf
    cs_s[...] = (cf.astype(F32) * scale).astype(BF)
    kern[...] = mm(cf, b_s[...], 1, 1) * scale

    for load in loads[3:5]:
        load.wait()
    total = cumb[rows - 1 : rows, :]
    rg[...] = (jnp.exp(cumb[...]) * g[...].astype(F32)).astype(BF)
    xw[...] = (jnp.exp(total - cumb[...]) * x[...].astype(F32)).astype(BF)
    f_fresh[...] = mm(b_s[...], xw[...], 0, 0)
    r_fresh[...] = mm(cs_s[...], rg[...], 0, 0)
    pl.semaphore_wait(barrier, group - 1 + n_z - 1)

    def chain(i, fresh, src, dst, to):
        return pltpu.make_async_remote_copy(
            src_ref=src, dst_ref=dst, send_sem=chain_send.at[i], recv_sem=chain_recv.at[i],
            device_id={"tm": to}, device_id_type=MESH,
        )

    up = lax.rem(tm + 1, n_tm)
    down = lax.rem(tm + n_tm - 1, n_tm)
    fwd = chain(0, f_fresh, f_out, f_in, up)
    rev = chain(1, r_fresh, r_out, r_in, down)

    def chain_step(copy, place, fresh, src, dst):
        @pl.when(place == 0)
        def _():
            dst[...] = jnp.zeros_like(dst)

        @pl.when(place > 0)
        def _():
            copy.wait_recv()

        @pl.when(place < n_tm - 1)
        def _():
            carried = jnp.exp(cumb[rows - 1 : rows, :])
            src[...] = (carried * dst[...].astype(F32) + fresh[...]).astype(BF)
            copy.start()

    rplace = n_tm - 1 - tm
    fslot = jnp.where(tm < 2, tm, 2 * tm - 1)
    rslot = jnp.where(rplace < 2, rplace, 2 * rplace - 1)

    halos = [
        pltpu.make_async_remote_copy(
            src_ref=buf.at[pl.ds(rows, W)], dst_ref=buf.at[pl.ds(0, W)],
            send_sem=halo_send.at[i], recv_sem=halo_recv.at[i],
            device_id={"tm": up}, device_id_type=MESH,
        )
        for i, buf in enumerate((kx, vx))
    ]
    per = 2 if heads % 2 == 0 else 1
    steps = heads // per
    wsum[...] = jnp.zeros_like(wsum)
    for load in loads[5:]:
        load.wait()

    def lanes(h):
        return pl.ds(pl.multiple_of(h * dim, dim), dim)

    def local_step(i, _):
        @pl.when(fslot == i)
        def _():
            chain_step(fwd, tm, f_fresh, f_out, f_in)

        @pl.when(rslot == i)
        def _():
            chain_step(rev, rplace, r_fresh, r_out, r_in)

        @pl.when((tm < n_tm - 1) & (i == min(1, steps - 1)))
        def _():
            for halo in halos:
                halo.start()

        acc = wsum[...]
        for j in range(per):
            h = i * per + j
            at = lanes(h)
            cb = cumb[:, at]
            gap = jnp.concatenate([cb] * (rows // dim), axis=1) - cumt[pl.ds(h, 1), :]
            decay = jnp.exp(jnp.where(row_i >= col_i, gap, -jnp.inf))
            mixing = (kern[...] * decay).astype(BF)
            xh, gh = x[:, at], g[:, at]
            acc = acc + mm(gh, xh, 1, 1) * decay
            inner[:, at] = mm(mixing, xh)
            gx[:, at] = mm(mixing, gh, 0, 0)
        wsum[...] = acc
        return 0

    lax.fori_loop(0, steps, local_step, 0)

    @pl.when(fslot >= steps)
    def _():
        chain_step(fwd, tm, f_fresh, f_out, f_in)

    @pl.when(rslot >= steps)
    def _():
        chain_step(rev, rplace, r_fresh, r_out, r_in)

    weigh = (wsum[...] * scale).astype(BF)
    both[:, :states] = (mm(weigh, c_s[...], 0, 0) + mm(xw[...], r_in[...], 1, 1)).astype(BF)
    both[:, states:] = (
        mm(weigh, b_s[...]) + mm(rg[...], f_in[...], 1, 1) * scale
    ).astype(BF)
    zscatter = []
    for k in range(1, n_z):
        other, to = zmember(k)
        zscatter.append(
            pltpu.make_async_remote_copy(
                src_ref=both.at[pl.ds(pl.multiple_of(other * zrows, zrows), zrows)],
                dst_ref=rz.at[k - 1], send_sem=zs_send.at[k - 1], recv_sem=zs_recv.at[k - 1],
                device_id=to, device_id_type=MESH,
            )
        )
        zscatter[-1].start()

    a_row = lax.broadcasted_iota(jnp.int32, (QB, W + QB), 0)
    a_col = lax.broadcasted_iota(jnp.int32, (QB, W + QB), 1)

    def attend(blk):
        seen = (a_col <= a_row + W) & (a_col >= a_row + 1 + off_ref[0, blk])
        seen = seen & (a_col >= W - (tm * rows + blk * QB))

        def step(i, _):
            for j in range(per):
                at = lanes(i * per + j)
                s = mm(q[blk * QB : (blk + 1) * QB, at], kx[blk * QB : blk * QB + W + QB, at], 1, 1)
                s = jnp.where(seen, s, -jnp.inf)
                top = jnp.max(s, axis=1, keepdims=True)
                e = jnp.exp((s - top) * (1.0 / math.sqrt(dim)))
                whole = jnp.sum(e, axis=1, keepdims=True)
                o = mm(e.astype(BF), vx[blk * QB : blk * QB + W + QB, at])
                att[blk * QB : (blk + 1) * QB, at] = o / whole
            return 0

        lax.fori_loop(0, steps, step, 0)

    for blk in range(1, rows // QB):
        attend(blk)

    mine = pl.ds(pl.multiple_of(z * zrows, zrows), zrows)
    for copy in zscatter:
        copy.wait_recv()
    part = both[mine, :].astype(F32)
    for k in range(n_z - 1):
        part = part + rz[k].astype(F32)
    zfull[mine, :] = part.astype(BF)
    zgather = []
    for k in range(1, n_z):
        other, to = zmember(k)
        zgather.append(
            pltpu.make_async_remote_copy(
                src_ref=zfull.at[mine], dst_ref=zfull.at[mine],
                send_sem=zg_send.at[k - 1], recv_sem=zg_recv.at[k - 1],
                device_id=to, device_id_type=MESH,
            )
        )
        zgather[-1].start()

    @pl.when(tm > 0)
    def _():
        for halo in halos:
            halo.wait_recv()

    @pl.when(tm == 0)
    def _():
        for buf in (kx, vx):
            buf[0:W, :] = jnp.zeros((W, width), BF)

    attend(0)

    for copy in zgather:
        copy.wait_recv()
    cols = pl.ds(pl.multiple_of(z * share, share), share)
    grad = mm(lat[:, cols], zfull[...], 0, 0) * (1.0 / math.sqrt(n_dp * rows * n_tm))
    term[...] = grad.astype(BF)
    scatter = []
    for k in range(1, group):
        other, to = member(k)
        at = jnp.where(other < owners, other, 0) if owners < group else other
        copy = pltpu.make_async_remote_copy(
            src_ref=term.at[pl.ds(pl.multiple_of(at * chunk, chunk), chunk)],
            dst_ref=rs.at[k - 1], send_sem=rs_send.at[k - 1], recv_sem=rs_recv.at[k - 1],
            device_id=to, device_id_type=MESH,
        )
        scatter.append((other < owners, copy))

    def when(cond, action):
        if owners == group:
            action()
        else:
            pl.when(cond)(action)

    for cond, copy in scatter:
        when(cond, copy.start)

    def finish(i, _):
        for j in range(per):
            at = lanes(i * per + j)
            cb = cumb[:, at]
            out = inner[:, at] + jnp.exp(cb) * mm(cs_s[...], f_in[:, at])
            mean = jnp.mean(out * out, axis=1, keepdims=True)
            lo[:, at] = (out * lax.rsqrt(mean + 1e-05) + att[:, at]).astype(BF)
            fall = jnp.exp(cb[rows - 1 : rows, :] - cb)
            ig[:, at] = (gx[:, at] + fall * mm(b_s[...], r_in[:, at])).astype(BF)
        return 0

    lax.fori_loop(0, steps, finish, 0)
    stores = [
        pltpu.make_async_copy(src, dst, store_sem.at[i])
        for i, (src, dst) in enumerate([(lo, lo_h), (ig, ig_h), (pg, pg_h)])
    ]
    stores[0].start()
    stores[1].start()

    own = jnp.where(me < owners, me, 0) if owners < group else me
    owned = pl.ds(pl.multiple_of(own * chunk, chunk), chunk)
    gather = []
    for k in range(1, group):
        other, to = member(k)
        copy = pltpu.make_async_remote_copy(
            src_ref=agf.at[owned], dst_ref=agf.at[owned],
            send_sem=ag_send.at[k - 1], recv_sem=ag_recv.at[k - 1],
            device_id=to, device_id_type=MESH,
        )
        gather.append((lax.rem(me + group - k, group) < owners, copy))

    def own_sum():
        for _, copy in scatter:
            copy.wait_recv()
        part = term[owned, :].astype(F32)
        for k in range(group - 1):
            part = part + rs[k].astype(F32)
        agf[owned, :] = part.astype(BF)
        for _, copy in gather:
            copy.start()

    when(me < owners, own_sum)
    for cond, copy in gather:
        when(cond, copy.wait_recv)
    pg[...] = agf[...].astype(F32)
    stores[2].start()

    for copy in zscatter + zgather:
        copy.wait_send()
    for cond, copy in scatter:
        when(cond, copy.wait_send)

    def gathered():
        for _, copy in gather:
            copy.wait_send()

    when(me < owners, gathered)

    @pl.when(tm < n_tm - 1)
    def _():
        fwd.wait_send()
        for halo in halos:
            halo.wait_send()

    @pl.when(tm > 0)
    def _():
        rev.wait_send()

    for store in stores:
        store.wait()


def on_device(
    sizes,
    latents,
    proj_input,
    proj_output,
    scan_input,
    log_decay,
    att_queries,
    att_keys,
    att_values,
    scan_cotangent,
    window_offsets,
):
    n_tm, n_z, n_dp = sizes
    clips, rows, model = latents.shape
    assert clips == 1
    width = scan_input.shape[2]
    heads = log_decay.shape[2]
    states = proj_input.shape[1]
    share = model // n_z
    group = n_tm * n_dp
    owners = min(group, share // 16)
    chunk = share // owners
    zrows = rows // n_z
    hbm = pl.BlockSpec(memory_space=pl.ANY)
    vmem = pl.BlockSpec(memory_space=pltpu.VMEM)
    smem = pl.BlockSpec(memory_space=pltpu.SMEM)

    def v(shape, kind=BF):
        return pltpu.VMEM(shape, kind)

    dma = pltpu.SemaphoreType.DMA
    layer_out, input_grad, proj_grad = pl.pallas_call(
        functools.partial(kernel, sizes),
        out_shape=(
            jax.ShapeDtypeStruct((rows, width), BF),
            jax.ShapeDtypeStruct((rows, width), BF),
            jax.ShapeDtypeStruct((share, 2 * states), F32),
        ),
        in_specs=[hbm, hbm, hbm, hbm, vmem, hbm, hbm, hbm, hbm, smem],
        out_specs=(hbm, hbm, hbm),
        scratch_shapes=[
            v((rows, model)), v((model, states)), v((model, states)),
            v((rows, width)), v((rows, width)), v((rows, width)),
            v((W + rows, width)), v((W + rows, width)),
            v((rows, width)), v((rows, width)), v((share, 2 * states), F32),
            v((rows, width), F32), v((heads, rows), F32),
            v((rows, states)), v((rows, states)), v((rows, states)),
            v((rows, rows), F32), v((rows, rows), F32),
            v((rows, width)), v((rows, width)),
            v((rows, width), F32), v((rows, width), F32), v((rows, width), F32),
            v((states, width), F32), v((states, width)), v((states, width)),
            v((states, width), F32), v((states, width)), v((states, width)),
            v((rows, 2 * states)), v((n_z - 1, zrows, 2 * states)), v((rows, 2 * states)),
            v((share, 2 * states)), v((group - 1, chunk, 2 * states)), v((share, 2 * states)),
            dma((8,)), dma((3,)), dma((2,)), dma((2,)), dma((2,)), dma((2,)),
            dma((n_z - 1,)), dma((n_z - 1,)), dma((n_z - 1,)), dma((n_z - 1,)),
            dma((group - 1,)), dma((group - 1,)), dma((group - 1,)), dma((group - 1,)),
        ],
        compiler_params=pltpu.CompilerParams(
            collective_id=0, has_side_effects=True, vmem_limit_bytes=48 * 1024 * 1024
        ),
    )(
        latents[0], proj_input, proj_output, scan_input[0], log_decay[0],
        att_queries[0], att_keys[0], att_values[0], scan_cotangent[0], window_offsets,
    )
    return layer_out[None], input_grad[None], proj_grad


def solution(mesh):
    sizes = (mesh.shape["tm"], mesh.shape["space"], mesh.shape["dp"])
    return jax.shard_map(
        functools.partial(on_device, sizes),
        mesh=mesh,
        in_specs=(
            P("dp", "tm", None),
            P(),
            P(),
            P("dp", "tm", "space"),
            P("dp", "tm", "space"),
            P("dp", "tm", "space"),
            P("dp", "tm", "space"),
            P("dp", "tm", "space"),
            P("dp", "tm", "space"),
            P("dp", "tm"),
        ),
        out_specs=(P("dp", "tm", "space"), P("dp", "tm", "space"), P("space", None)),
        check_vma=False,
    )
```

```python
import functools
import math

import jax
import jax.numpy as jnp
from jax import lax
from jax.experimental import pallas as pl
from jax.experimental.pallas import tpu as pltpu
from jax.sharding import PartitionSpec as P

W = 128
QB = 128
MESH = pl.DeviceIdType.MESH
BF = jnp.bfloat16
F32 = jnp.float32


def mm(a, b, ca=1, cb=0):
    return lax.dot_general(a, b, (((ca,), (cb,)), ((), ())), preferred_element_type=F32)


def three(a):
    first = a.astype(BF).astype(F32)
    second = (a - first).astype(BF).astype(F32)
    return jnp.concatenate([first, second, a - first - second], axis=0).astype(BF)


def kernel(
    sizes,
    lat_h, pi_h, po_h, x_h, ld_ref, q_h, k_h, v_h, g_h, off_ref,
    lo_h, ig_h, pg_h,
    lat, pi, po, x, g, q, kx, vx, lo, ig, lat_t,
    cumb, cumt, b_s, c_s, cs_s, kern, wsum, xw, rg, inner, gx, att,
    f_fresh, f_in, f_out, r_fresh, r_in, r_out,
    both, rz, zfull, term, rs, agf,
    load_sem, store_sem, chain_send, chain_recv, halo_send, halo_recv,
    zs_send, zs_recv, zg_send, zg_recv, rs_send, rs_recv, ag_send, ag_recv,
):
    n_tm, n_z, n_dp = sizes
    rows, width = x.shape
    heads = ld_ref.shape[0]
    dim = width // heads
    states = pi.shape[1]
    scale = 1.0 / math.sqrt(states)
    group = n_tm * n_dp
    share = lat.shape[1] // n_z
    owners = min(group, share // 16)
    chunk = share // owners
    zrows = rows // n_z
    tm = lax.axis_index("tm")
    z = lax.axis_index("space")
    dp = lax.axis_index("dp")
    me = dp * n_tm + tm

    def member(k):
        other = lax.rem(me + k, group)
        return other, {"dp": other // n_tm, "tm": lax.rem(other, n_tm)}

    def zmember(k):
        other = lax.rem(z + k, n_z)
        return other, {"space": other}

    loads = [
        pltpu.make_async_copy(src, dst, load_sem.at[i])
        for i, (src, dst) in enumerate(
            [
                (lat_h, lat), (pi_h, pi), (po_h, po), (x_h, x), (g_h, g),
                (k_h, kx.at[pl.ds(W, rows)]), (v_h, vx.at[pl.ds(W, rows)]), (q_h, q),
            ]
        )
    ]
    for load in loads:
        load.start()

    barrier = pltpu.get_barrier_semaphore()
    for k in range(1, group):
        pl.semaphore_signal(barrier, inc=1, device_id=member(k)[1], device_id_type=MESH)
    for k in range(1, n_z):
        pl.semaphore_signal(barrier, inc=1, device_id=zmember(k)[1], device_id_type=MESH)

    row_i = lax.broadcasted_iota(jnp.int32, (rows, rows), 0)
    col_i = lax.broadcasted_iota(jnp.int32, (rows, rows), 1)
    upper = (row_i <= col_i).astype(BF)
    sums = mm(three(ld_ref[...]), upper)
    cum = sums[:heads] + sums[heads : 2 * heads] + sums[2 * heads :]
    cumt[...] = cum
    spread = (
        lax.broadcasted_iota(jnp.int32, (3 * heads, width), 1) // dim
        == lax.rem(lax.broadcasted_iota(jnp.int32, (3 * heads, width), 0), heads)
    ).astype(BF)
    cumb[...] = mm(three(cum), spread, 0, 0)

    for load in loads[:3]:
        load.wait()
    b_s[...] = mm(lat[...], pi[...]).astype(BF)
    cf = mm(lat[...], po[...]).astype(BF)
    c_s[...] = cf
    cs_s[...] = (cf.astype(F32) * scale).astype(BF)
    kern[...] = mm(cf, b_s[...], 1, 1) * scale

    for load in loads[3:5]:
        load.wait()
    total = cumb[rows - 1 : rows, :]
    rg[...] = (jnp.exp(cumb[...]) * g[...].astype(F32)).astype(BF)
    xw[...] = (jnp.exp(total - cumb[...]) * x[...].astype(F32)).astype(BF)
    f_fresh[...] = mm(b_s[...], xw[...], 0, 0)
    r_fresh[...] = mm(cs_s[...], rg[...], 0, 0)
    pl.semaphore_wait(barrier, group - 1 + n_z - 1)

    def chain(i, fresh, src, dst, to):
        return pltpu.make_async_remote_copy(
            src_ref=src, dst_ref=dst, send_sem=chain_send.at[i], recv_sem=chain_recv.at[i],
            device_id={"tm": to}, device_id_type=MESH,
        )

    up = lax.rem(tm + 1, n_tm)
    down = lax.rem(tm + n_tm - 1, n_tm)
    fwd = chain(0, f_fresh, f_out, f_in, up)
    rev = chain(1, r_fresh, r_out, r_in, down)

    def chain_step(copy, place, fresh, src, dst):
        @pl.when(place == 0)
        def _():
            dst[...] = jnp.zeros_like(dst)

        @pl.when(place > 0)
        def _():
            copy.wait_recv()

        @pl.when(place < n_tm - 1)
        def _():
            carried = jnp.exp(cumb[rows - 1 : rows, :])
            src[...] = (carried * dst[...].astype(F32) + fresh[...]).astype(BF)
            copy.start()

    rplace = n_tm - 1 - tm
    fslot = jnp.where(tm < 2, tm, 2 * tm - 1)
    rslot = jnp.where(rplace < 2, rplace, 2 * rplace - 1)

    halos = [
        pltpu.make_async_remote_copy(
            src_ref=buf.at[pl.ds(rows, W)], dst_ref=buf.at[pl.ds(0, W)],
            send_sem=halo_send.at[i], recv_sem=halo_recv.at[i],
            device_id={"tm": up}, device_id_type=MESH,
        )
        for i, buf in enumerate((kx, vx))
    ]
    per = 2 if heads % 2 == 0 else 1
    steps = heads // per
    wsum[...] = jnp.zeros_like(wsum)
    for load in loads[5:]:
        load.wait()

    def lanes(h):
        return pl.ds(pl.multiple_of(h * dim, dim), dim)

    def local_step(i, _):
        @pl.when(fslot == i)
        def _():
            chain_step(fwd, tm, f_fresh, f_out, f_in)

        @pl.when(rslot == i)
        def _():
            chain_step(rev, rplace, r_fresh, r_out, r_in)

        acc = wsum[...]
        for j in range(per):
            h = i * per + j
            at = lanes(h)
            cb = cumb[:, at]
            gap = jnp.concatenate([cb] * (rows // dim), axis=1) - cumt[pl.ds(h, 1), :]
            decay = jnp.exp(jnp.where(row_i >= col_i, gap, -jnp.inf))
            mixing = (kern[...] * decay).astype(BF)
            xh, gh = x[:, at], g[:, at]
            acc = acc + mm(gh, xh, 1, 1) * decay
            inner[:, at] = mm(mixing, xh)
            gx[:, at] = mm(mixing, gh, 0, 0)
        wsum[...] = acc
        return 0

    lax.fori_loop(0, steps, local_step, 0)

    @pl.when(fslot >= steps)
    def _():
        chain_step(fwd, tm, f_fresh, f_out, f_in)

    @pl.when(rslot >= steps)
    def _():
        chain_step(rev, rplace, r_fresh, r_out, r_in)

    weigh = (wsum[...] * scale).astype(BF)
    halves = (1, 0)
    half_at = [pl.ds(0, states), pl.ds(states, states)]
    zscatter, zgather, scatter, gather = {}, {}, {}, {}
    mine = pl.ds(pl.multiple_of(z * zrows, zrows), zrows)
    for half in halves:
        if half:
            rows_grad = mm(weigh, b_s[...]) + mm(rg[...], f_in[...], 1, 1) * scale
        else:
            rows_grad = mm(weigh, c_s[...], 0, 0) + mm(xw[...], r_in[...], 1, 1)
        both[:, half_at[half]] = rows_grad.astype(BF)
        zscatter[half] = []
        for k in range(1, n_z):
            other, to = zmember(k)
            zscatter[half].append(
                pltpu.make_async_remote_copy(
                    src_ref=both.at[
                        pl.ds(pl.multiple_of(other * zrows, zrows), zrows), half_at[half]
                    ],
                    dst_ref=rz.at[half, k - 1],
                    send_sem=zs_send.at[half, k - 1],
                    recv_sem=zs_recv.at[half, k - 1],
                    device_id=to, device_id_type=MESH,
                )
            )
            zscatter[half][-1].start()

    @pl.when(tm < n_tm - 1)
    def _():
        for halo in halos:
            halo.start()

    a_row = lax.broadcasted_iota(jnp.int32, (QB, W + QB), 0)
    a_col = lax.broadcasted_iota(jnp.int32, (QB, W + QB), 1)

    def attend(blk, put):
        seen = (a_col <= a_row + W) & (a_col >= a_row + 1 + off_ref[0, blk])
        seen = seen & (a_col >= W - (tm * rows + blk * QB))

        def step(i, _):
            for j in range(per):
                at = lanes(i * per + j)
                s = mm(q[blk * QB : (blk + 1) * QB, at], kx[blk * QB : blk * QB + W + QB, at], 1, 1)
                s = jnp.where(seen, s, -jnp.inf)
                top = jnp.max(s, axis=1, keepdims=True)
                e = jnp.exp((s - top) * (1.0 / math.sqrt(dim)))
                whole = jnp.sum(e, axis=1, keepdims=True)
                o = mm(e.astype(BF), vx[blk * QB : blk * QB + W + QB, at])
                put(at, o / whole)
            return 0

        lax.fori_loop(0, steps, step, 0)

    for blk in range(1, rows // QB):
        def keep(at, o, blk=blk):
            att[blk * QB : (blk + 1) * QB, at] = o

        attend(blk, keep)
    cols = pl.ds(pl.multiple_of(z * share, share), share)
    lat_t[...] = lat[:, cols].T

    for half in halves:
        for copy in zscatter[half]:
            copy.wait_recv()
        part = both[mine, half_at[half]].astype(F32)
        for k in range(n_z - 1):
            part = part + rz[half, k].astype(F32)
        zfull[mine, half_at[half]] = part.astype(BF)
        zgather[half] = []
        for k in range(1, n_z):
            other, to = zmember(k)
            zgather[half].append(
                pltpu.make_async_remote_copy(
                    src_ref=zfull.at[mine, half_at[half]],
                    dst_ref=zfull.at[mine, half_at[half]],
                    send_sem=zg_send.at[half, k - 1],
                    recv_sem=zg_recv.at[half, k - 1],
                    device_id=to, device_id_type=MESH,
                )
            )
            zgather[half][-1].start()

    def finish(i, _):
        for j in range(per):
            at = lanes(i * per + j)
            cb = cumb[:, at]
            out = inner[:, at] + jnp.exp(cb) * mm(cs_s[...], f_in[:, at])
            mean = jnp.mean(out * out, axis=1, keepdims=True)
            normed = out * lax.rsqrt(mean + 1e-05)
            inner[0:QB, at] = normed[0:QB]
            lo[QB:rows, at] = (normed[QB:rows] + att[QB:rows, at]).astype(BF)
            fall = jnp.exp(cb[rows - 1 : rows, :] - cb)
            ig[:, at] = (gx[:, at] + fall * mm(b_s[...], r_in[:, at])).astype(BF)
        return 0

    lax.fori_loop(0, steps, finish, 0)
    stores = [
        pltpu.make_async_copy(src, dst, store_sem.at[i])
        for i, (src, dst) in enumerate([(lo, lo_h), (ig, ig_h), (agf, pg_h)])
    ]
    stores[1].start()

    def when(cond, action):
        if owners == group:
            action()
        else:
            pl.when(cond)(action)

    for half in halves:
        for copy in zgather[half]:
            copy.wait_recv()
        grad = mm(lat_t[...], zfull[:, half_at[half]])
        term[:, half_at[half]] = (grad * (1.0 / math.sqrt(n_dp * rows * n_tm))).astype(BF)
        scatter[half] = []
        for k in range(1, group):
            other, to = member(k)
            at = jnp.where(other < owners, other, 0) if owners < group else other
            copy = pltpu.make_async_remote_copy(
                src_ref=term.at[pl.ds(pl.multiple_of(at * chunk, chunk), chunk), half_at[half]],
                dst_ref=rs.at[half, k - 1],
                send_sem=rs_send.at[half, k - 1],
                recv_sem=rs_recv.at[half, k - 1],
                device_id=to, device_id_type=MESH,
            )
            scatter[half].append((other < owners, copy))
            when(other < owners, copy.start)

    @pl.when(tm > 0)
    def _():
        for halo in halos:
            halo.wait_recv()

    @pl.when(tm == 0)
    def _():
        for buf in (kx, vx):
            buf[0:W, :] = jnp.zeros((W, width), BF)

    def add(at, o):
        lo[0:QB, at] = (inner[0:QB, at] + o).astype(BF)

    attend(0, add)
    stores[0].start()

    own = jnp.where(me < owners, me, 0) if owners < group else me
    owned = pl.ds(pl.multiple_of(own * chunk, chunk), chunk)

    def own_sum(half):
        for _, copy in scatter[half]:
            copy.wait_recv()
        part = term[owned, half_at[half]].astype(F32)
        for k in range(group - 1):
            part = part + rs[half, k].astype(F32)
        agf[owned, half_at[half]] = part.astype(BF)
        for _, copy in gather[half]:
            copy.start()

    for half in halves:
        gather[half] = []
        for k in range(1, group):
            other, to = member(k)
            copy = pltpu.make_async_remote_copy(
                src_ref=agf.at[owned, half_at[half]],
                dst_ref=agf.at[owned, half_at[half]],
                send_sem=ag_send.at[half, k - 1],
                recv_sem=ag_recv.at[half, k - 1],
                device_id=to, device_id_type=MESH,
            )
            gather[half].append((lax.rem(me + group - k, group) < owners, copy))
        when(me < owners, functools.partial(own_sum, half))

    @pl.when(tm < n_tm - 1)
    def _():
        fwd.wait_send()
        for halo in halos:
            halo.wait_send()

    @pl.when(tm > 0)
    def _():
        rev.wait_send()

    def gathered(half):
        for _, copy in gather[half]:
            copy.wait_send()

    for half in halves:
        for copy in zscatter[half] + zgather[half]:
            copy.wait_send()
        for cond, copy in scatter[half]:
            when(cond, copy.wait_send)
    for half in halves:
        for cond, copy in gather[half]:
            when(cond, copy.wait_recv)
        when(me < owners, functools.partial(gathered, half))
    stores[2].start()
    for store in stores:
        store.wait()


def on_device(
    sizes,
    latents,
    proj_input,
    proj_output,
    scan_input,
    log_decay,
    att_queries,
    att_keys,
    att_values,
    scan_cotangent,
    window_offsets,
):
    n_tm, n_z, n_dp = sizes
    clips, rows, model = latents.shape
    assert clips == 1
    width = scan_input.shape[2]
    heads = log_decay.shape[2]
    states = proj_input.shape[1]
    share = model // n_z
    group = n_tm * n_dp
    owners = min(group, share // 16)
    chunk = share // owners
    zrows = rows // n_z
    hbm = pl.BlockSpec(memory_space=pltpu.HBM)
    anywhere = pl.BlockSpec(memory_space=pl.ANY)
    vmem = pl.BlockSpec(memory_space=pltpu.VMEM)
    smem = pl.BlockSpec(memory_space=pltpu.SMEM)

    def v(shape, kind=BF):
        return pltpu.VMEM(shape, kind)

    dma = pltpu.SemaphoreType.DMA
    layer_out, input_grad, proj_grad = pl.pallas_call(
        functools.partial(kernel, sizes),
        out_shape=(
            jax.ShapeDtypeStruct((rows, width), BF),
            jax.ShapeDtypeStruct((rows, width), BF),
            jax.ShapeDtypeStruct((share, 2 * states), BF),
        ),
        in_specs=[hbm, hbm, hbm, hbm, vmem, hbm, hbm, hbm, hbm, smem],
        out_specs=(anywhere, anywhere, anywhere),
        scratch_shapes=[
            v((rows, model)), v((model, states)), v((model, states)),
            v((rows, width)), v((rows, width)), v((rows, width)),
            v((W + rows, width)), v((W + rows, width)),
            v((rows, width)), v((rows, width)), v((share, rows)),
            v((rows, width), F32), v((heads, rows), F32),
            v((rows, states)), v((rows, states)), v((rows, states)),
            v((rows, rows), F32), v((rows, rows), F32),
            v((rows, width)), v((rows, width)),
            v((rows, width), F32), v((rows, width), F32), v((rows, width), F32),
            v((states, width), F32), v((states, width)), v((states, width)),
            v((states, width), F32), v((states, width)), v((states, width)),
            v((rows, 2 * states)), v((2, n_z - 1, zrows, states)), v((rows, 2 * states)),
            v((share, 2 * states)), v((2, group - 1, chunk, states)), v((share, 2 * states)),
            dma((8,)), dma((3,)), dma((2,)), dma((2,)), dma((2,)), dma((2,)),
            dma((2, n_z - 1)), dma((2, n_z - 1)), dma((2, n_z - 1)), dma((2, n_z - 1)),
            dma((2, group - 1)), dma((2, group - 1)), dma((2, group - 1)), dma((2, group - 1)),
        ],
        compiler_params=pltpu.CompilerParams(
            collective_id=0, has_side_effects=True, vmem_limit_bytes=60 * 1024 * 1024
        ),
    )(
        latents[0], proj_input, proj_output, scan_input[0], log_decay[0].T,
        att_queries[0], att_keys[0], att_values[0], scan_cotangent[0], window_offsets,
    )
    return layer_out[None], input_grad[None], proj_grad.astype(F32)


def solution(mesh):
    sizes = (mesh.shape["tm"], mesh.shape["space"], mesh.shape["dp"])
    return jax.shard_map(
        functools.partial(on_device, sizes),
        mesh=mesh,
        in_specs=(
            P("dp", "tm", None),
            P(),
            P(),
            P("dp", "tm", "space"),
            P("dp", "tm", "space"),
            P("dp", "tm", "space"),
            P("dp", "tm", "space"),
            P("dp", "tm", "space"),
            P("dp", "tm", "space"),
            P("dp", "tm"),
        ),
        out_specs=(P("dp", "tm", "space"), P("dp", "tm", "space"), P("space", None)),
        check_vma=False,
    )
```

```python
import functools
import math

import jax
import jax.numpy as jnp
from jax import lax
from jax.experimental import pallas as pl
from jax.experimental.pallas import tpu as pltpu
from jax.sharding import PartitionSpec as P

W = 128
QB = 128
MESH = pl.DeviceIdType.MESH
BF = jnp.bfloat16
F32 = jnp.float32


def mm(a, b, ca=1, cb=0):
    return lax.dot_general(a, b, (((ca,), (cb,)), ((), ())), preferred_element_type=F32)


def three(a):
    first = a.astype(BF).astype(F32)
    second = (a - first).astype(BF).astype(F32)
    return jnp.concatenate([first, second, a - first - second], axis=0).astype(BF)


def kernel(
    sizes,
    lat_h, pi_h, po_h, x_h, ld_ref, q_h, k_h, v_h, g_h, off_ref,
    lo_h, ig_h, pg_h,
    lat, pi, po, x, g, q, kx, vx, lo, ig, lat_t,
    cumb, cumt, b_s, c_s, cs_s, kern, wsum, xw, rg, inner, gx, att,
    f_fresh, f_in, f_out, r_fresh, r_in, r_out,
    both, rz, zfull, term, rs, agf,
    load_sem, store_sem, chain_send, chain_recv, halo_send, halo_recv,
    zs_send, zs_recv, zg_send, zg_recv, rs_send, rs_recv, ag_send, ag_recv,
):
    n_tm, n_z, n_dp = sizes
    rows, width = x.shape
    heads = ld_ref.shape[0]
    dim = width // heads
    states = pi.shape[1]
    scale = 1.0 / math.sqrt(states)
    group = n_tm * n_dp
    share = lat.shape[1] // n_z
    owners = min(group, share // 16)
    chunk = share // owners
    zrows = rows // n_z
    tm = lax.axis_index("tm")
    z = lax.axis_index("space")
    dp = lax.axis_index("dp")
    me = dp * n_tm + tm

    def member(k):
        other = lax.rem(me + k, group)
        return other, {"dp": other // n_tm, "tm": lax.rem(other, n_tm)}

    def zmember(k):
        other = lax.rem(z + k, n_z)
        return other, {"space": other}

    loads = [
        pltpu.make_async_copy(src, dst, load_sem.at[i])
        for i, (src, dst) in enumerate(
            [
                (lat_h, lat), (pi_h, pi), (po_h, po), (x_h, x), (g_h, g),
                (k_h, kx.at[pl.ds(W, rows)]), (v_h, vx.at[pl.ds(W, rows)]), (q_h, q),
            ]
        )
    ]
    for load in loads:
        load.start()

    barrier = pltpu.get_barrier_semaphore()
    for k in range(1, group):
        pl.semaphore_signal(barrier, inc=1, device_id=member(k)[1], device_id_type=MESH)
    for k in range(1, n_z):
        pl.semaphore_signal(barrier, inc=1, device_id=zmember(k)[1], device_id_type=MESH)

    row_i = lax.broadcasted_iota(jnp.int32, (rows, rows), 0)
    col_i = lax.broadcasted_iota(jnp.int32, (rows, rows), 1)
    upper = (row_i <= col_i).astype(BF)
    sums = mm(three(ld_ref[...]), upper)
    cum = sums[:heads] + sums[heads : 2 * heads] + sums[2 * heads :]
    cumt[...] = cum
    spread = (
        lax.broadcasted_iota(jnp.int32, (3 * heads, width), 1) // dim
        == lax.rem(lax.broadcasted_iota(jnp.int32, (3 * heads, width), 0), heads)
    ).astype(BF)
    cumb[...] = mm(three(cum), spread, 0, 0)

    for load in loads[:3]:
        load.wait()
    b_s[...] = mm(lat[...], pi[...]).astype(BF)
    cf = mm(lat[...], po[...]).astype(BF)
    c_s[...] = cf
    cs_s[...] = (cf.astype(F32) * scale).astype(BF)
    kern[...] = mm(cf, b_s[...], 1, 1) * scale

    for load in loads[3:5]:
        load.wait()
    total = cumb[rows - 1 : rows, :]
    rg[...] = (jnp.exp(cumb[...]) * g[...].astype(F32)).astype(BF)
    xw[...] = (jnp.exp(total - cumb[...]) * x[...].astype(F32)).astype(BF)
    f_fresh[...] = mm(b_s[...], xw[...], 0, 0)
    r_fresh[...] = mm(cs_s[...], rg[...], 0, 0)
    pl.semaphore_wait(barrier, group - 1 + n_z - 1)

    def chain(i, fresh, src, dst, to):
        return pltpu.make_async_remote_copy(
            src_ref=src, dst_ref=dst, send_sem=chain_send.at[i], recv_sem=chain_recv.at[i],
            device_id={"tm": to}, device_id_type=MESH,
        )

    up = lax.rem(tm + 1, n_tm)
    down = lax.rem(tm + n_tm - 1, n_tm)
    fwd = chain(0, f_fresh, f_out, f_in, up)
    rev = chain(1, r_fresh, r_out, r_in, down)

    def chain_step(copy, place, fresh, src, dst):
        @pl.when(place == 0)
        def _():
            dst[...] = jnp.zeros_like(dst)

        @pl.when(place > 0)
        def _():
            copy.wait_recv()

        @pl.when(place < n_tm - 1)
        def _():
            carried = jnp.exp(cumb[rows - 1 : rows, :])
            src[...] = (carried * dst[...].astype(F32) + fresh[...]).astype(BF)
            copy.start()

    rplace = n_tm - 1 - tm
    early_fwd = 2 * tm < n_tm
    half_of = [jnp.where(early_fwd, 1, 0), jnp.where(early_fwd, 0, 1)]

    def early_step(ready):
        @pl.when(early_fwd & ready(tm))
        def _():
            chain_step(fwd, tm, f_fresh, f_out, f_in)

        @pl.when(jnp.logical_not(early_fwd) & ready(rplace))
        def _():
            chain_step(rev, rplace, r_fresh, r_out, r_in)

    def late_step(ready):
        @pl.when(early_fwd & ready(rplace))
        def _():
            chain_step(rev, rplace, r_fresh, r_out, r_in)

        @pl.when(jnp.logical_not(early_fwd) & ready(tm))
        def _():
            chain_step(fwd, tm, f_fresh, f_out, f_in)

    halos = [
        pltpu.make_async_remote_copy(
            src_ref=buf.at[pl.ds(rows, W)], dst_ref=buf.at[pl.ds(0, W)],
            send_sem=halo_send.at[i], recv_sem=halo_recv.at[i],
            device_id={"tm": up}, device_id_type=MESH,
        )
        for i, buf in enumerate((kx, vx))
    ]
    per = 2 if heads % 2 == 0 else 1
    steps = heads // per
    wsum[...] = jnp.zeros_like(wsum)
    for load in loads[5:]:
        load.wait()

    def lanes(h):
        return pl.ds(pl.multiple_of(h * dim, dim), dim)

    def local_step(i, _):
        early_step(lambda place: place == i)

        acc = wsum[...]
        for j in range(per):
            h = i * per + j
            at = lanes(h)
            cb = cumb[:, at]
            gap = jnp.concatenate([cb] * (rows // dim), axis=1) - cumt[pl.ds(h, 1), :]
            decay = jnp.exp(jnp.where(row_i >= col_i, gap, -jnp.inf))
            mixing = (kern[...] * decay).astype(BF)
            xh, gh = x[:, at], g[:, at]
            acc = acc + mm(gh, xh, 1, 1) * decay
            inner[:, at] = mm(mixing, xh)
            gx[:, at] = mm(mixing, gh, 0, 0)
        wsum[...] = acc
        return 0

    lax.fori_loop(0, steps, local_step, 0)

    early_step(lambda place: place >= steps)

    weigh = (wsum[...] * scale).astype(BF)
    zscatter, zgather, scatter, gather = [[], []], [[], []], [[], []], [[], []]
    mine = pl.ds(pl.multiple_of(z * zrows, zrows), zrows)
    cols = pl.ds(pl.multiple_of(z * share, share), share)

    def fill_c():
        both[1] = (mm(weigh, b_s[...]) + mm(rg[...], f_in[...], 1, 1) * scale).astype(BF)

    def fill_b():
        both[0] = (mm(weigh, c_s[...], 0, 0) + mm(xw[...], r_in[...], 1, 1)).astype(BF)

    def start_zscatter(turn):
        c_now = early_fwd if turn == 0 else jnp.logical_not(early_fwd)
        pl.when(c_now)(fill_c)
        pl.when(jnp.logical_not(c_now))(fill_b)
        half = half_of[turn]
        for k in range(1, n_z):
            other, to = zmember(k)
            copy = pltpu.make_async_remote_copy(
                src_ref=both.at[half, pl.ds(pl.multiple_of(other * zrows, zrows), zrows)],
                dst_ref=rz.at[half, k - 1],
                send_sem=zs_send.at[half, k - 1],
                recv_sem=zs_recv.at[half, k - 1],
                device_id=to, device_id_type=MESH,
            )
            zscatter[turn].append(copy)
            copy.start()

    def start_zgather(turn):
        half = half_of[turn]
        for copy in zscatter[turn]:
            copy.wait_recv()
        part = both[half, mine, :].astype(F32)
        for k in range(n_z - 1):
            part = part + rz[half, k].astype(F32)
        zfull[half, mine, :] = part.astype(BF)
        for k in range(1, n_z):
            other, to = zmember(k)
            copy = pltpu.make_async_remote_copy(
                src_ref=zfull.at[half, mine],
                dst_ref=zfull.at[half, mine],
                send_sem=zg_send.at[half, k - 1],
                recv_sem=zg_recv.at[half, k - 1],
                device_id=to, device_id_type=MESH,
            )
            zgather[turn].append(copy)
            copy.start()

    def when(cond, action):
        if owners == group:
            action()
        else:
            pl.when(cond)(action)

    def start_scatter(turn):
        half = half_of[turn]
        for copy in zgather[turn]:
            copy.wait_recv()
        grad = mm(lat_t[...], zfull[half])
        term[half] = (grad * (1.0 / math.sqrt(n_dp * rows * n_tm))).astype(BF)
        for k in range(1, group):
            other, to = member(k)
            at = jnp.where(other < owners, other, 0) if owners < group else other
            copy = pltpu.make_async_remote_copy(
                src_ref=term.at[half, pl.ds(pl.multiple_of(at * chunk, chunk), chunk)],
                dst_ref=rs.at[half, k - 1],
                send_sem=rs_send.at[half, k - 1],
                recv_sem=rs_recv.at[half, k - 1],
                device_id=to, device_id_type=MESH,
            )
            scatter[turn].append((other < owners, copy))
            when(other < owners, copy.start)

    a_row = lax.broadcasted_iota(jnp.int32, (QB, W + QB), 0)
    a_col = lax.broadcasted_iota(jnp.int32, (QB, W + QB), 1)

    def attend(blk, put, low, high):
        seen = (a_col <= a_row + W) & (a_col >= a_row + 1 + off_ref[0, blk])
        seen = seen & (a_col >= W - (tm * rows + blk * QB))

        def step(i, _):
            for j in range(per):
                at = lanes(i * per + j)
                s = mm(q[blk * QB : (blk + 1) * QB, at], kx[blk * QB : blk * QB + W + QB, at], 1, 1)
                s = jnp.where(seen, s, -jnp.inf)
                top = jnp.max(s, axis=1, keepdims=True)
                e = jnp.exp((s - top) * (1.0 / math.sqrt(dim)))
                whole = jnp.sum(e, axis=1, keepdims=True)
                o = mm(e.astype(BF), vx[blk * QB : blk * QB + W + QB, at])
                put(at, o / whole)
            return 0

        lax.fori_loop(low, high, step, 0)

    def attend_own(low, high):
        for blk in range(1, rows // QB):
            def keep(at, o, blk=blk):
                att[blk * QB : (blk + 1) * QB, at] = o

            attend(blk, keep, low, high)

    def finish(i, _):
        for j in range(per):
            at = lanes(i * per + j)
            cb = cumb[:, at]
            out = inner[:, at] + jnp.exp(cb) * mm(cs_s[...], f_in[:, at])
            mean = jnp.mean(out * out, axis=1, keepdims=True)
            normed = out * lax.rsqrt(mean + 1e-05)
            inner[0:QB, at] = normed[0:QB]
            lo[QB:rows, at] = (normed[QB:rows] + att[QB:rows, at]).astype(BF)
            fall = jnp.exp(cb[rows - 1 : rows, :] - cb)
            ig[:, at] = (gx[:, at] + fall * mm(b_s[...], r_in[:, at])).astype(BF)
        return 0

    def add(at, o):
        lo[0:QB, at] = (inner[0:QB, at] + o).astype(BF)

    stores = [
        pltpu.make_async_copy(src, dst, store_sem.at[i])
        for i, (src, dst) in enumerate([(lo, lo_h), (ig, ig_h), (agf, pg_h)])
    ]

    start_zscatter(0)

    @pl.when(tm < n_tm - 1)
    def _():
        for halo in halos:
            halo.start()

    attend_own(0, steps // 2)
    late_step(lambda place: place <= 2)
    attend_own(steps // 2, steps)
    lat_t[...] = lat[:, cols].T
    start_zgather(0)
    late_step(lambda place: place > 2)
    start_zscatter(1)
    start_scatter(0)
    lax.fori_loop(0, steps // 2, finish, 0)
    start_zgather(1)
    lax.fori_loop(steps // 2, steps, finish, 0)
    stores[1].start()

    @pl.when(tm > 0)
    def _():
        for halo in halos:
            halo.wait_recv()

    @pl.when(tm == 0)
    def _():
        for buf in (kx, vx):
            buf[0:W, :] = jnp.zeros((W, width), BF)

    start_scatter(1)
    attend(0, add, 0, steps)
    stores[0].start()

    own = jnp.where(me < owners, me, 0) if owners < group else me
    owned = pl.ds(pl.multiple_of(own * chunk, chunk), chunk)
    for copies in scatter:
        for _, copy in copies:
            when(me < owners, copy.wait_recv)
    for half in range(2):
        for k in range(1, group):
            other, to = member(k)
            copy = pltpu.make_async_remote_copy(
                src_ref=agf.at[half, owned],
                dst_ref=agf.at[half, owned],
                send_sem=ag_send.at[half, k - 1],
                recv_sem=ag_recv.at[half, k - 1],
                device_id=to, device_id_type=MESH,
            )
            gather[half].append((lax.rem(me + group - k, group) < owners, copy))

        def own_sum(half=half):
            part = term[half, owned, :].astype(F32)
            for k in range(group - 1):
                part = part + rs[half, k].astype(F32)
            agf[half, owned, :] = part.astype(BF)
            for _, copy in gather[half]:
                copy.start()

        when(me < owners, own_sum)

    @pl.when(tm < n_tm - 1)
    def _():
        fwd.wait_send()
        for halo in halos:
            halo.wait_send()

    @pl.when(tm > 0)
    def _():
        rev.wait_send()

    for turn in range(2):
        for copy in zscatter[turn] + zgather[turn]:
            copy.wait_send()
        for cond, copy in scatter[turn]:
            when(cond, copy.wait_send)
    for half in range(2):
        for cond, copy in gather[half]:
            when(cond, copy.wait_recv)
    stores[2].start()
    for half in range(2):
        for _, copy in gather[half]:
            when(me < owners, copy.wait_send)
    for store in stores:
        store.wait()


def hand_out(lo_h, ig_h, pg_ref, lo_out, ig_out, pg_out, sem):
    copies = [
        pltpu.make_async_copy(lo_h, lo_out, sem.at[0]),
        pltpu.make_async_copy(ig_h, ig_out, sem.at[1]),
    ]
    for copy in copies:
        copy.start()
    for half in range(2):
        states = pg_ref.shape[2]
        pg_out[:, half * states : (half + 1) * states] = pg_ref[half].astype(F32)
    for copy in copies:
        copy.wait()


def on_device(
    sizes,
    latents,
    proj_input,
    proj_output,
    scan_input,
    log_decay,
    att_queries,
    att_keys,
    att_values,
    scan_cotangent,
    window_offsets,
):
    n_tm, n_z, n_dp = sizes
    clips, rows, model = latents.shape
    assert clips == 1
    width = scan_input.shape[2]
    heads = log_decay.shape[2]
    states = proj_input.shape[1]
    share = model // n_z
    group = n_tm * n_dp
    owners = min(group, share // 16)
    chunk = share // owners
    zrows = rows // n_z
    hbm = pl.BlockSpec(memory_space=pltpu.HBM)
    anywhere = pl.BlockSpec(memory_space=pl.ANY)
    vmem = pl.BlockSpec(memory_space=pltpu.VMEM)
    smem = pl.BlockSpec(memory_space=pltpu.SMEM)

    def v(shape, kind=BF):
        return pltpu.VMEM(shape, kind)

    dma = pltpu.SemaphoreType.DMA
    layer_out, input_grad, proj_grad = pl.pallas_call(
        functools.partial(kernel, sizes),
        out_shape=(
            jax.ShapeDtypeStruct((rows, width), BF),
            jax.ShapeDtypeStruct((rows, width), BF),
            jax.ShapeDtypeStruct((2, share, states), BF),
        ),
        in_specs=[hbm, hbm, hbm, hbm, vmem, hbm, hbm, hbm, hbm, smem],
        out_specs=(anywhere, anywhere, anywhere),
        scratch_shapes=[
            v((rows, model)), v((model, states)), v((model, states)),
            v((rows, width)), v((rows, width)), v((rows, width)),
            v((W + rows, width)), v((W + rows, width)),
            v((rows, width)), v((rows, width)), v((share, rows)),
            v((rows, width), F32), v((heads, rows), F32),
            v((rows, states)), v((rows, states)), v((rows, states)),
            v((rows, rows), F32), v((rows, rows), F32),
            v((rows, width)), v((rows, width)),
            v((rows, width), F32), v((rows, width), F32), v((rows, width), F32),
            v((states, width), F32), v((states, width)), v((states, width)),
            v((states, width), F32), v((states, width)), v((states, width)),
            v((2, rows, states)), v((2, n_z - 1, zrows, states)), v((2, rows, states)),
            v((2, share, states)), v((2, group - 1, chunk, states)), v((2, share, states)),
            dma((8,)), dma((3,)), dma((2,)), dma((2,)), dma((2,)), dma((2,)),
            dma((2, n_z - 1)), dma((2, n_z - 1)), dma((2, n_z - 1)), dma((2, n_z - 1)),
            dma((2, group - 1)), dma((2, group - 1)), dma((2, group - 1)), dma((2, group - 1)),
        ],
        compiler_params=pltpu.CompilerParams(
            collective_id=0, has_side_effects=True, vmem_limit_bytes=60 * 1024 * 1024
        ),
    )(
        latents[0], proj_input, proj_output, scan_input[0], log_decay[0].T,
        att_queries[0], att_keys[0], att_values[0], scan_cotangent[0], window_offsets,
    )
    layer_out, input_grad, proj_grad = pl.pallas_call(
        hand_out,
        out_shape=(
            jax.ShapeDtypeStruct((rows, width), BF),
            jax.ShapeDtypeStruct((rows, width), BF),
            jax.ShapeDtypeStruct((share, 2 * states), F32),
        ),
        in_specs=[hbm, hbm, vmem],
        out_specs=(hbm, hbm, vmem),
        scratch_shapes=[dma((2,))],
        compiler_params=pltpu.CompilerParams(vmem_limit_bytes=60 * 1024 * 1024),
    )(layer_out, input_grad, proj_grad)
    return layer_out[None], input_grad[None], proj_grad


def solution(mesh):
    sizes = (mesh.shape["tm"], mesh.shape["space"], mesh.shape["dp"])
    return jax.shard_map(
        functools.partial(on_device, sizes),
        mesh=mesh,
        in_specs=(
            P("dp", "tm", None),
            P(),
            P(),
            P("dp", "tm", "space"),
            P("dp", "tm", "space"),
            P("dp", "tm", "space"),
            P("dp", "tm", "space"),
            P("dp", "tm", "space"),
            P("dp", "tm", "space"),
            P("dp", "tm"),
        ),
        out_specs=(P("dp", "tm", "space"), P("dp", "tm", "space"), P("space", None)),
        check_vma=False,
    )
```

```python
import functools
import math

import jax
import jax.numpy as jnp
from jax import lax
from jax.experimental import pallas as pl
from jax.experimental.pallas import tpu as pltpu
from jax.sharding import PartitionSpec as P

W = 128
QB = 128
MESH = pl.DeviceIdType.MESH
BF = jnp.bfloat16
F32 = jnp.float32


def mm(a, b, ca=1, cb=0):
    return lax.dot_general(a, b, (((ca,), (cb,)), ((), ())), preferred_element_type=F32)


def three(a):
    first = a.astype(BF).astype(F32)
    second = (a - first).astype(BF).astype(F32)
    return jnp.concatenate([first, second, a - first - second], axis=0).astype(BF)


def kernel(
    sizes,
    lat_h, pi_h, po_h, x_h, ld_ref, q_h, k_h, v_h, g_h, off_ref,
    lo_h, ig_h, pg_h,
    lat, proj, x, g, q, kx, vx, lo, ig, lat_t,
    cumb, cumt, b_s, c_s, cs_s, kern, wsum, xw, rg, inner, gx, att,
    f_fresh, f_in, f_out, r_fresh, r_in, r_out,
    both, rz, zfull, term, rs, agf,
    load_sem, store_sem, chain_send, chain_recv, halo_send, halo_recv,
    zs_send, zs_recv, zg_send, zg_recv, rs_send, rs_recv, ag_send, ag_recv,
):
    n_tm, n_z, n_dp = sizes
    rows, width = x.shape
    heads = ld_ref.shape[0]
    dim = width // heads
    states = proj.shape[1] // 2
    scale = 1.0 / math.sqrt(states)
    group = n_tm * n_dp
    share = lat.shape[1] // n_z
    owners = min(group, share // 16)
    chunk = share // owners
    zrows = rows // n_z
    tm = lax.axis_index("tm")
    z = lax.axis_index("space")
    dp = lax.axis_index("dp")
    me = dp * n_tm + tm

    def member(k):
        other = lax.rem(me + k, group)
        return other, {"dp": other // n_tm, "tm": lax.rem(other, n_tm)}

    def zmember(k):
        other = lax.rem(z + k, n_z)
        return other, {"space": other}

    loads = [
        pltpu.make_async_copy(src, dst, load_sem.at[i])
        for i, (src, dst) in enumerate(
            [
                (lat_h, lat), (pi_h, proj.at[:, 0:states]),
                (po_h, proj.at[:, states : 2 * states]), (x_h, x), (g_h, g),
                (k_h, kx.at[pl.ds(W, rows)]), (v_h, vx.at[pl.ds(W, rows)]), (q_h, q),
            ]
        )
    ]
    for load in loads:
        load.start()

    barrier = pltpu.get_barrier_semaphore()
    for k in range(1, group):
        pl.semaphore_signal(barrier, inc=1, device_id=member(k)[1], device_id_type=MESH)
    for k in range(1, n_z):
        pl.semaphore_signal(barrier, inc=1, device_id=zmember(k)[1], device_id_type=MESH)

    row_i = lax.broadcasted_iota(jnp.int32, (rows, rows), 0)
    col_i = lax.broadcasted_iota(jnp.int32, (rows, rows), 1)
    upper = (row_i <= col_i).astype(BF)
    sums = mm(three(ld_ref[...]), upper)
    cum = sums[:heads] + sums[heads : 2 * heads] + sums[2 * heads :]
    cumt[...] = cum
    spread = (
        lax.broadcasted_iota(jnp.int32, (3 * heads, width), 1) // dim
        == lax.rem(lax.broadcasted_iota(jnp.int32, (3 * heads, width), 0), heads)
    ).astype(BF)
    cumb[...] = mm(three(cum), spread, 0, 0)

    for load in loads[:3]:
        load.wait()
    bc = mm(lat[...], proj[...]).astype(BF)
    b_s[...] = bc[:, :states]
    c_s[...] = bc[:, states:]
    cs_s[...] = (bc[:, states:].astype(F32) * scale).astype(BF)

    for load in loads[3:5]:
        load.wait()
    total = cumb[rows - 1 : rows, :]
    rg[...] = (jnp.exp(cumb[...]) * g[...].astype(F32)).astype(BF)
    xw[...] = (jnp.exp(total - cumb[...]) * x[...].astype(F32)).astype(BF)
    f_fresh[...] = mm(b_s[...], xw[...], 0, 0)
    r_fresh[...] = mm(cs_s[...], rg[...], 0, 0)
    pl.semaphore_wait(barrier, group - 1 + n_z - 1)

    def chain(i, fresh, src, dst, to):
        return pltpu.make_async_remote_copy(
            src_ref=src, dst_ref=dst, send_sem=chain_send.at[i], recv_sem=chain_recv.at[i],
            device_id={"tm": to}, device_id_type=MESH,
        )

    up = lax.rem(tm + 1, n_tm)
    down = lax.rem(tm + n_tm - 1, n_tm)
    fwd = chain(0, f_fresh, f_out, f_in, up)
    rev = chain(1, r_fresh, r_out, r_in, down)

    def chain_step(copy, place, fresh, src, dst):
        @pl.when(place == 0)
        def _():
            dst[...] = jnp.zeros_like(dst)

        @pl.when(place > 0)
        def _():
            copy.wait_recv()

        @pl.when(place < n_tm - 1)
        def _():
            carried = jnp.exp(cumb[rows - 1 : rows, :])
            src[...] = (carried * dst[...].astype(F32) + fresh[...]).astype(BF)
            copy.start()

    rplace = n_tm - 1 - tm
    early_fwd = 2 * tm < n_tm
    half_of = [jnp.where(early_fwd, 1, 0), jnp.where(early_fwd, 0, 1)]

    def early_step(ready):
        @pl.when(early_fwd & ready(tm))
        def _():
            chain_step(fwd, tm, f_fresh, f_out, f_in)

        @pl.when(jnp.logical_not(early_fwd) & ready(rplace))
        def _():
            chain_step(rev, rplace, r_fresh, r_out, r_in)

    def late_step(ready):
        @pl.when(early_fwd & ready(rplace))
        def _():
            chain_step(rev, rplace, r_fresh, r_out, r_in)

        @pl.when(jnp.logical_not(early_fwd) & ready(tm))
        def _():
            chain_step(fwd, tm, f_fresh, f_out, f_in)

    halos = [
        pltpu.make_async_remote_copy(
            src_ref=buf.at[pl.ds(rows, W)], dst_ref=buf.at[pl.ds(0, W)],
            send_sem=halo_send.at[i], recv_sem=halo_recv.at[i],
            device_id={"tm": up}, device_id_type=MESH,
        )
        for i, buf in enumerate((kx, vx))
    ]
    per = 4 if heads % 4 == 0 else heads
    steps = heads // per
    early_step(lambda place: place == 0)
    kern[...] = mm(cs_s[...], b_s[...], 1, 1)
    wsum[...] = jnp.zeros_like(wsum)
    for load in loads[5:]:
        load.wait()

    assert rows == 2 * dim
    tri = lax.broadcasted_iota(jnp.int32, (dim, dim), 0) >= lax.broadcasted_iota(
        jnp.int32, (dim, dim), 1
    )

    def lanes(h):
        return pl.ds(pl.multiple_of(h * dim, dim), dim)

    def local_step(i, _):
        early_step(lambda place: (place == i) & (i > 0))

        w00, w10, w11 = wsum[:dim, :dim], wsum[dim:, :dim], wsum[dim:, dim:]
        for j in range(per):
            h = i * per + j
            at = lanes(h)
            ct = cumt[pl.ds(h, 1), :]
            cb0, cb1 = cumb[:dim, at], cumb[dim:, at]
            d00 = jnp.exp(jnp.where(tri, cb0 - ct[:, :dim], -jnp.inf))
            d10 = jnp.exp(cb1 - ct[:, :dim])
            d11 = jnp.exp(jnp.where(tri, cb1 - ct[:, dim:], -jnp.inf))
            m00 = (kern[:dim, :dim] * d00).astype(BF)
            m10 = (kern[dim:, :dim] * d10).astype(BF)
            m11 = (kern[dim:, dim:] * d11).astype(BF)
            xh, gh = x[:, at], g[:, at]
            p00 = mm(gh[:dim], xh[:dim], 1, 1)
            p1 = mm(gh[dim:], xh, 1, 1)
            w00 = w00 + p00 * d00
            w10 = w10 + p1[:, :dim] * d10
            w11 = w11 + p1[:, dim:] * d11
            inner[:dim, at] = mm(m00, xh[:dim])
            inner[dim:, at] = mm(jnp.concatenate([m10, m11], axis=1), xh)
            gx[:dim, at] = mm(jnp.concatenate([m00, m10], axis=0), gh, 0, 0)
            gx[dim:, at] = mm(m11, gh[dim:], 0, 0)
        wsum[:dim, :dim] = w00
        wsum[dim:, :dim] = w10
        wsum[dim:, dim:] = w11
        return 0

    lax.fori_loop(0, steps, local_step, 0)

    early_step(lambda place: place >= steps)

    weigh = (wsum[...] * scale).astype(BF)
    zscatter, zgather, scatter, gather = [[], []], [[], []], [[], []], [[], []]
    mine = pl.ds(pl.multiple_of(z * zrows, zrows), zrows)
    cols = pl.ds(pl.multiple_of(z * share, share), share)

    def fill_c():
        both[1] = (mm(weigh, b_s[...]) + mm(rg[...], f_in[...], 1, 1) * scale).astype(BF)

    def fill_b():
        both[0] = (mm(weigh, c_s[...], 0, 0) + mm(xw[...], r_in[...], 1, 1)).astype(BF)

    def start_zscatter(turn):
        c_now = early_fwd if turn == 0 else jnp.logical_not(early_fwd)
        pl.when(c_now)(fill_c)
        pl.when(jnp.logical_not(c_now))(fill_b)
        half = half_of[turn]
        for k in range(1, n_z):
            other, to = zmember(k)
            copy = pltpu.make_async_remote_copy(
                src_ref=both.at[half, pl.ds(pl.multiple_of(other * zrows, zrows), zrows)],
                dst_ref=rz.at[half, k - 1],
                send_sem=zs_send.at[half, k - 1],
                recv_sem=zs_recv.at[half, k - 1],
                device_id=to, device_id_type=MESH,
            )
            zscatter[turn].append(copy)
            copy.start()

    def start_zgather(turn):
        half = half_of[turn]
        for copy in zscatter[turn]:
            copy.wait_recv()
        part = both[half, mine, :].astype(F32)
        for k in range(n_z - 1):
            part = part + rz[half, k].astype(F32)
        zfull[half, mine, :] = part.astype(BF)
        for k in range(1, n_z):
            other, to = zmember(k)
            copy = pltpu.make_async_remote_copy(
                src_ref=zfull.at[half, mine],
                dst_ref=zfull.at[half, mine],
                send_sem=zg_send.at[half, k - 1],
                recv_sem=zg_recv.at[half, k - 1],
                device_id=to, device_id_type=MESH,
            )
            zgather[turn].append(copy)
            copy.start()

    def when(cond, action):
        if owners == group:
            action()
        else:
            pl.when(cond)(action)

    def start_scatter(turn):
        half = half_of[turn]
        for copy in zgather[turn]:
            copy.wait_recv()
        grad = mm(lat_t[...], zfull[half])
        term[half] = (grad * (1.0 / math.sqrt(n_dp * rows * n_tm))).astype(BF)
        for k in range(1, group):
            other, to = member(k)
            at = jnp.where(other < owners, other, 0) if owners < group else other
            copy = pltpu.make_async_remote_copy(
                src_ref=term.at[half, pl.ds(pl.multiple_of(at * chunk, chunk), chunk)],
                dst_ref=rs.at[half, k - 1],
                send_sem=rs_send.at[half, k - 1],
                recv_sem=rs_recv.at[half, k - 1],
                device_id=to, device_id_type=MESH,
            )
            scatter[turn].append((other < owners, copy))
            when(other < owners, copy.start)

    a_row = lax.broadcasted_iota(jnp.int32, (QB, W + QB), 0)
    a_col = lax.broadcasted_iota(jnp.int32, (QB, W + QB), 1)

    def attend(blk, put, low, high):
        seen = (a_col <= a_row + W) & (a_col >= a_row + 1 + off_ref[0, blk])
        seen = seen & (a_col >= W - (tm * rows + blk * QB))

        def step(i, _):
            for j in range(per):
                at = lanes(i * per + j)
                s = mm(q[blk * QB : (blk + 1) * QB, at], kx[blk * QB : blk * QB + W + QB, at], 1, 1)
                s = jnp.where(seen, s, -jnp.inf)
                top = jnp.max(s, axis=1, keepdims=True)
                e = jnp.exp((s - top) * (1.0 / math.sqrt(dim)))
                whole = jnp.sum(e, axis=1, keepdims=True)
                o = mm(e.astype(BF), vx[blk * QB : blk * QB + W + QB, at])
                put(at, o / whole)
            return 0

        lax.fori_loop(low, high, step, 0)

    def attend_own(low, high):
        for blk in range(1, rows // QB):
            def keep(at, o, blk=blk):
                att[blk * QB : (blk + 1) * QB, at] = o

            attend(blk, keep, low, high)

    def finish(i, _):
        for j in range(per):
            at = lanes(i * per + j)
            cb = cumb[:, at]
            out = inner[:, at] + jnp.exp(cb) * mm(cs_s[...], f_in[:, at])
            mean = jnp.mean(out * out, axis=1, keepdims=True)
            normed = out * lax.rsqrt(mean + 1e-05)
            inner[0:QB, at] = normed[0:QB]
            lo[QB:rows, at] = (normed[QB:rows] + att[QB:rows, at]).astype(BF)
            fall = jnp.exp(cb[rows - 1 : rows, :] - cb)
            ig[:, at] = (gx[:, at] + fall * mm(b_s[...], r_in[:, at])).astype(BF)
        return 0

    def add(at, o):
        lo[0:QB, at] = (inner[0:QB, at] + o).astype(BF)

    stores = [
        pltpu.make_async_copy(src, dst, store_sem.at[i])
        for i, (src, dst) in enumerate([(lo, lo_h), (ig, ig_h), (agf, pg_h)])
    ]

    start_zscatter(0)

    @pl.when(tm < n_tm - 1)
    def _():
        for halo in halos:
            halo.start()

    attend_own(0, steps // 2)
    late_step(lambda place: place <= 2)
    attend_own(steps // 2, steps)
    lat_t[...] = lat[:, cols].T
    start_zgather(0)
    late_step(lambda place: place > 2)
    start_zscatter(1)
    start_scatter(0)
    lax.fori_loop(0, steps // 2, finish, 0)
    start_zgather(1)
    lax.fori_loop(steps // 2, steps, finish, 0)
    stores[1].start()

    @pl.when(tm > 0)
    def _():
        for halo in halos:
            halo.wait_recv()

    @pl.when(tm == 0)
    def _():
        for buf in (kx, vx):
            buf[0:W, :] = jnp.zeros((W, width), BF)

    start_scatter(1)
    attend(0, add, 0, (steps + 1) // 2)

    own = jnp.where(me < owners, me, 0) if owners < group else me
    owned = pl.ds(pl.multiple_of(own * chunk, chunk), chunk)
    for copies in scatter:
        for _, copy in copies:
            when(me < owners, copy.wait_recv)
    for half in range(2):
        for k in range(1, group):
            other, to = member(k)
            copy = pltpu.make_async_remote_copy(
                src_ref=agf.at[half, owned],
                dst_ref=agf.at[half, owned],
                send_sem=ag_send.at[half, k - 1],
                recv_sem=ag_recv.at[half, k - 1],
                device_id=to, device_id_type=MESH,
            )
            gather[half].append((lax.rem(me + group - k, group) < owners, copy))

        def own_sum(half=half):
            part = term[half, owned, :].astype(F32)
            for k in range(group - 1):
                part = part + rs[half, k].astype(F32)
            agf[half, owned, :] = part.astype(BF)
            for _, copy in gather[half]:
                copy.start()

        when(me < owners, own_sum)

    attend(0, add, (steps + 1) // 2, steps)
    stores[0].start()

    @pl.when(tm < n_tm - 1)
    def _():
        fwd.wait_send()
        for halo in halos:
            halo.wait_send()

    @pl.when(tm > 0)
    def _():
        rev.wait_send()

    for turn in range(2):
        for copy in zscatter[turn] + zgather[turn]:
            copy.wait_send()
        for cond, copy in scatter[turn]:
            when(cond, copy.wait_send)
    for half in range(2):
        for cond, copy in gather[half]:
            when(cond, copy.wait_recv)
    stores[2].start()
    for half in range(2):
        for _, copy in gather[half]:
            when(me < owners, copy.wait_send)
    for store in stores:
        store.wait()


def hand_out(lo_ref, ig_ref, pg_ref, lo_out, ig_out, pg_out, pg, sem):
    copies = [
        pltpu.make_async_copy(src, dst, sem.at[i])
        for i, (src, dst) in enumerate([(lo_ref, lo_out), (ig_ref, ig_out), (pg, pg_out)])
    ]
    copies[0].start()
    copies[1].start()
    states = pg_ref.shape[2]
    for half in range(2):
        pg[:, half * states : (half + 1) * states] = pg_ref[half].astype(F32)
    copies[2].start()
    for copy in copies:
        copy.wait()


def on_device(
    sizes,
    latents,
    proj_input,
    proj_output,
    scan_input,
    log_decay,
    att_queries,
    att_keys,
    att_values,
    scan_cotangent,
    window_offsets,
):
    n_tm, n_z, n_dp = sizes
    clips, rows, model = latents.shape
    assert clips == 1
    width = scan_input.shape[2]
    heads = log_decay.shape[2]
    states = proj_input.shape[1]
    share = model // n_z
    group = n_tm * n_dp
    owners = min(group, share // 16)
    chunk = share // owners
    zrows = rows // n_z
    hbm = pl.BlockSpec(memory_space=pltpu.HBM)
    anywhere = pl.BlockSpec(memory_space=pl.ANY)
    vmem = pl.BlockSpec(memory_space=pltpu.VMEM)
    smem = pl.BlockSpec(memory_space=pltpu.SMEM)

    def v(shape, kind=BF):
        return pltpu.VMEM(shape, kind)

    dma = pltpu.SemaphoreType.DMA
    layer_out, input_grad, proj_grad = pl.pallas_call(
        functools.partial(kernel, sizes),
        out_shape=(
            jax.ShapeDtypeStruct((rows, width), BF),
            jax.ShapeDtypeStruct((rows, width), BF),
            jax.ShapeDtypeStruct((2, share, states), BF),
        ),
        in_specs=[hbm, hbm, hbm, hbm, vmem, hbm, hbm, hbm, hbm, smem],
        out_specs=(anywhere, anywhere, anywhere),
        scratch_shapes=[
            v((rows, model)), v((model, 2 * states)),
            v((rows, width)), v((rows, width)), v((rows, width)),
            v((W + rows, width)), v((W + rows, width)),
            v((rows, width)), v((rows, width)), v((share, rows)),
            v((rows, width), F32), v((heads, rows), F32),
            v((rows, states)), v((rows, states)), v((rows, states)),
            v((rows, rows), F32), v((rows, rows), F32),
            v((rows, width)), v((rows, width)),
            v((rows, width), F32), v((rows, width), F32), v((rows, width), F32),
            v((states, width), F32), v((states, width)), v((states, width)),
            v((states, width), F32), v((states, width)), v((states, width)),
            v((2, rows, states)), v((2, n_z - 1, zrows, states)), v((2, rows, states)),
            v((2, share, states)), v((2, group - 1, chunk, states)), v((2, share, states)),
            dma((8,)), dma((3,)), dma((2,)), dma((2,)), dma((2,)), dma((2,)),
            dma((2, n_z - 1)), dma((2, n_z - 1)), dma((2, n_z - 1)), dma((2, n_z - 1)),
            dma((2, group - 1)), dma((2, group - 1)), dma((2, group - 1)), dma((2, group - 1)),
        ],
        compiler_params=pltpu.CompilerParams(
            collective_id=0, has_side_effects=True, vmem_limit_bytes=60 * 1024 * 1024
        ),
    )(
        latents[0], proj_input, proj_output, scan_input[0], log_decay[0].T,
        att_queries[0], att_keys[0], att_values[0], scan_cotangent[0], window_offsets,
    )
    layer_out, input_grad, proj_grad = pl.pallas_call(
        hand_out,
        out_shape=(
            jax.ShapeDtypeStruct((rows, width), BF),
            jax.ShapeDtypeStruct((rows, width), BF),
            jax.ShapeDtypeStruct((share, 2 * states), F32),
        ),
        in_specs=[vmem, vmem, vmem],
        out_specs=(hbm, hbm, hbm),
        scratch_shapes=[v((share, 2 * states), F32), dma((3,))],
        compiler_params=pltpu.CompilerParams(vmem_limit_bytes=60 * 1024 * 1024),
    )(layer_out, input_grad, proj_grad)
    return layer_out[None], input_grad[None], proj_grad


def solution(mesh):
    sizes = (mesh.shape["tm"], mesh.shape["space"], mesh.shape["dp"])
    return jax.shard_map(
        functools.partial(on_device, sizes),
        mesh=mesh,
        in_specs=(
            P("dp", "tm", None),
            P(),
            P(),
            P("dp", "tm", "space"),
            P("dp", "tm", "space"),
            P("dp", "tm", "space"),
            P("dp", "tm", "space"),
            P("dp", "tm", "space"),
            P("dp", "tm", "space"),
            P("dp", "tm"),
        ),
        out_specs=(P("dp", "tm", "space"), P("dp", "tm", "space"), P("space", None)),
        check_vma=False,
    )
```

```python
import functools
import math

import jax
import jax.numpy as jnp
from jax import lax
from jax.experimental import pallas as pl
from jax.experimental.pallas import tpu as pltpu
from jax.sharding import PartitionSpec as P

W = 128
QB = 128
MESH = pl.DeviceIdType.MESH
BF = jnp.bfloat16
F32 = jnp.float32


def mm(a, b, ca=1, cb=0):
    return lax.dot_general(a, b, (((ca,), (cb,)), ((), ())), preferred_element_type=F32)


def three(a):
    first = a.astype(BF).astype(F32)
    second = (a - first).astype(BF).astype(F32)
    return jnp.concatenate([first, second, a - first - second], axis=0).astype(BF)


def kernel(
    sizes,
    lat_h, pi_h, po_h, x_h, ld_ref, q_h, k_h, v_h, g_h, off_ref,
    lo, ig, pg_out,
    lat, proj, x, g, q, kx, vx, lat_t,
    cumb, cumt, b_s, c_s, cs_s, kern, wsum, xw, rg, inner, gx, att,
    f_fresh, f_in, f_out, r_fresh, r_in, r_out,
    both, rz, zfull, term, rs, agf,
    load_sem, chain_send, chain_recv, halo_send, halo_recv,
    zs_send, zs_recv, zg_send, zg_recv, rs_send, rs_recv, ag_send, ag_recv,
):
    n_tm, n_z, n_dp = sizes
    rows, width = x.shape
    heads = ld_ref.shape[0]
    dim = width // heads
    states = proj.shape[1] // 2
    scale = 1.0 / math.sqrt(states)
    group = n_tm * n_dp
    share = lat.shape[1] // n_z
    owners = min(group, share // 16)
    chunk = share // owners
    zrows = rows // n_z
    tm = lax.axis_index("tm")
    z = lax.axis_index("space")
    dp = lax.axis_index("dp")
    me = dp * n_tm + tm

    def member(k):
        other = lax.rem(me + k, group)
        return other, {"dp": other // n_tm, "tm": lax.rem(other, n_tm)}

    def zmember(k):
        other = lax.rem(z + k, n_z)
        return other, {"space": other}

    loads = [
        pltpu.make_async_copy(src, dst, load_sem.at[i])
        for i, (src, dst) in enumerate(
            [
                (lat_h, lat), (pi_h, proj.at[:, 0:states]),
                (po_h, proj.at[:, states : 2 * states]), (x_h, x), (g_h, g),
                (k_h, kx.at[pl.ds(W, rows)]), (v_h, vx.at[pl.ds(W, rows)]), (q_h, q),
            ]
        )
    ]
    for load in loads[3:5] + loads[:3]:
        load.start()

    barrier = pltpu.get_barrier_semaphore()
    for k in range(1, group):
        pl.semaphore_signal(barrier, inc=1, device_id=member(k)[1], device_id_type=MESH)
    for k in range(1, n_z):
        pl.semaphore_signal(barrier, inc=1, device_id=zmember(k)[1], device_id_type=MESH)

    row_i = lax.broadcasted_iota(jnp.int32, (rows, rows), 0)
    col_i = lax.broadcasted_iota(jnp.int32, (rows, rows), 1)
    upper = (row_i <= col_i).astype(BF)
    sums = mm(three(ld_ref[...]), upper)
    cum = sums[:heads] + sums[heads : 2 * heads] + sums[2 * heads :]
    cumt[...] = cum
    spread = (
        lax.broadcasted_iota(jnp.int32, (3 * heads, width), 1) // dim
        == lax.rem(lax.broadcasted_iota(jnp.int32, (3 * heads, width), 0), heads)
    ).astype(BF)
    cumb[...] = mm(three(cum), spread, 0, 0)

    for load in loads[3:5]:
        load.wait()
    for load in loads[5:]:
        load.start()
    total = cumb[rows - 1 : rows, :]
    rg[...] = (jnp.exp(cumb[...]) * g[...].astype(F32)).astype(BF)
    xw[...] = (jnp.exp(total - cumb[...]) * x[...].astype(F32)).astype(BF)
    for load in loads[:3]:
        load.wait()
    bc = mm(lat[...], proj[...]).astype(BF)
    b_s[...] = bc[:, :states]
    c_s[...] = bc[:, states:]
    cs_s[...] = (bc[:, states:].astype(F32) * scale).astype(BF)
    f_fresh[...] = mm(b_s[...], xw[...], 0, 0)
    r_fresh[...] = mm(cs_s[...], rg[...], 0, 0)
    pl.semaphore_wait(barrier, group - 1 + n_z - 1)

    up = lax.rem(tm + 1, n_tm)
    down = lax.rem(tm + n_tm - 1, n_tm)
    pieces = [pl.ds(0, width // 2), pl.ds(width // 2, width // 2)]

    def chain(i, src, dst, to):
        return [
            pltpu.make_async_remote_copy(
                src_ref=src.at[:, at], dst_ref=dst.at[:, at],
                send_sem=chain_send.at[i, p], recv_sem=chain_recv.at[i, p],
                device_id={"tm": to}, device_id_type=MESH,
            )
            for p, at in enumerate(pieces)
        ]

    fwd = chain(0, f_out, f_in, up)
    rev = chain(1, r_out, r_in, down)

    def chain_step(copies, place, fresh, src, dst):
        @pl.when(place == 0)
        def _():
            dst[...] = jnp.zeros_like(dst)

        for copy, at in zip(copies, pieces):
            @pl.when(place > 0)
            def _(copy=copy):
                copy.wait_recv()

            @pl.when(place < n_tm - 1)
            def _(copy=copy, at=at):
                carried = jnp.exp(cumb[rows - 1 : rows, at])
                src[:, at] = (carried * dst[:, at].astype(F32) + fresh[:, at]).astype(BF)
                copy.start()

    rplace = n_tm - 1 - tm
    early_fwd = 2 * tm < n_tm
    half_of = [jnp.where(early_fwd, 1, 0), jnp.where(early_fwd, 0, 1)]

    def early_step(ready):
        @pl.when(early_fwd & ready(tm))
        def _():
            chain_step(fwd, tm, f_fresh, f_out, f_in)

        @pl.when(jnp.logical_not(early_fwd) & ready(rplace))
        def _():
            chain_step(rev, rplace, r_fresh, r_out, r_in)

    def late_step(ready):
        @pl.when(early_fwd & ready(rplace))
        def _():
            chain_step(rev, rplace, r_fresh, r_out, r_in)

        @pl.when(jnp.logical_not(early_fwd) & ready(tm))
        def _():
            chain_step(fwd, tm, f_fresh, f_out, f_in)

    halos = [
        pltpu.make_async_remote_copy(
            src_ref=buf.at[pl.ds(rows, W)], dst_ref=buf.at[pl.ds(0, W)],
            send_sem=halo_send.at[i], recv_sem=halo_recv.at[i],
            device_id={"tm": up}, device_id_type=MESH,
        )
        for i, buf in enumerate((kx, vx))
    ]
    per = 4 if heads % 4 == 0 else heads
    steps = heads // per
    early_step(lambda place: place == 0)
    kern[...] = mm(cs_s[...], b_s[...], 1, 1)
    wsum[...] = jnp.zeros_like(wsum)
    for load in loads[5:]:
        load.wait()

    assert rows == 2 * dim
    tri = lax.broadcasted_iota(jnp.int32, (dim, dim), 0) >= lax.broadcasted_iota(
        jnp.int32, (dim, dim), 1
    )

    def lanes(h):
        return pl.ds(pl.multiple_of(h * dim, dim), dim)

    def local_step(i, _):
        early_step(lambda place: (place == i) & (i > 0))

        w00, w10, w11 = wsum[:dim, :dim], wsum[dim:, :dim], wsum[dim:, dim:]
        for j in range(per):
            h = i * per + j
            at = lanes(h)
            ct = cumt[pl.ds(h, 1), :]
            cb0, cb1 = cumb[:dim, at], cumb[dim:, at]
            d00 = jnp.exp(jnp.where(tri, cb0 - ct[:, :dim], -jnp.inf))
            d10 = jnp.exp(cb1 - ct[:, :dim])
            d11 = jnp.exp(jnp.where(tri, cb1 - ct[:, dim:], -jnp.inf))
            m00 = (kern[:dim, :dim] * d00).astype(BF)
            m10 = (kern[dim:, :dim] * d10).astype(BF)
            m11 = (kern[dim:, dim:] * d11).astype(BF)
            xh, gh = x[:, at], g[:, at]
            p00 = mm(gh[:dim], xh[:dim], 1, 1)
            p1 = mm(gh[dim:], xh, 1, 1)
            w00 = w00 + p00 * d00
            w10 = w10 + p1[:, :dim] * d10
            w11 = w11 + p1[:, dim:] * d11
            inner[:dim, at] = mm(m00, xh[:dim])
            inner[dim:, at] = mm(jnp.concatenate([m10, m11], axis=1), xh)
            gx[:dim, at] = mm(jnp.concatenate([m00, m10], axis=0), gh, 0, 0)
            gx[dim:, at] = mm(m11, gh[dim:], 0, 0)
        wsum[:dim, :dim] = w00
        wsum[dim:, :dim] = w10
        wsum[dim:, dim:] = w11
        return 0

    lax.fori_loop(0, steps, local_step, 0)

    early_step(lambda place: place >= steps)

    weigh = (wsum[...] * scale).astype(BF)
    zscatter, zgather, scatter, gather = [[], []], [[], []], [[], []], [[], []]
    mine = pl.ds(pl.multiple_of(z * zrows, zrows), zrows)
    cols = pl.ds(pl.multiple_of(z * share, share), share)

    def fill_c():
        both[1] = (mm(weigh, b_s[...]) + mm(rg[...], f_in[...], 1, 1) * scale).astype(BF)

    def fill_b():
        both[0] = (mm(weigh, c_s[...], 0, 0) + mm(xw[...], r_in[...], 1, 1)).astype(BF)

    def start_zscatter(turn):
        c_now = early_fwd if turn == 0 else jnp.logical_not(early_fwd)
        pl.when(c_now)(fill_c)
        pl.when(jnp.logical_not(c_now))(fill_b)
        half = half_of[turn]
        for k in range(1, n_z):
            other, to = zmember(k)
            copy = pltpu.make_async_remote_copy(
                src_ref=both.at[half, pl.ds(pl.multiple_of(other * zrows, zrows), zrows)],
                dst_ref=rz.at[half, k - 1],
                send_sem=zs_send.at[half, k - 1],
                recv_sem=zs_recv.at[half, k - 1],
                device_id=to, device_id_type=MESH,
            )
            zscatter[turn].append(copy)
            copy.start()

    def start_zgather(turn):
        half = half_of[turn]
        for copy in zscatter[turn]:
            copy.wait_recv()
        part = both[half, mine, :].astype(F32)
        for k in range(n_z - 1):
            part = part + rz[half, k].astype(F32)
        zfull[half, mine, :] = part.astype(BF)
        for k in range(1, n_z):
            other, to = zmember(k)
            copy = pltpu.make_async_remote_copy(
                src_ref=zfull.at[half, mine],
                dst_ref=zfull.at[half, mine],
                send_sem=zg_send.at[half, k - 1],
                recv_sem=zg_recv.at[half, k - 1],
                device_id=to, device_id_type=MESH,
            )
            zgather[turn].append(copy)
            copy.start()

    def when(cond, action):
        if owners == group:
            action()
        else:
            pl.when(cond)(action)

    def start_scatter(turn):
        half = half_of[turn]
        for copy in zgather[turn]:
            copy.wait_recv()
        grad = mm(lat_t[...], zfull[half])
        term[half] = (grad * (1.0 / math.sqrt(n_dp * rows * n_tm))).astype(BF)
        for k in range(1, group):
            other, to = member(k)
            at = jnp.where(other < owners, other, 0) if owners < group else other
            copy = pltpu.make_async_remote_copy(
                src_ref=term.at[half, pl.ds(pl.multiple_of(at * chunk, chunk), chunk)],
                dst_ref=rs.at[half, k - 1],
                send_sem=rs_send.at[half, k - 1],
                recv_sem=rs_recv.at[half, k - 1],
                device_id=to, device_id_type=MESH,
            )
            scatter[turn].append((other < owners, copy))
            when(other < owners, copy.start)

    a_row = lax.broadcasted_iota(jnp.int32, (QB, W + QB), 0)
    a_col = lax.broadcasted_iota(jnp.int32, (QB, W + QB), 1)

    def attend(blk, put, low, high):
        seen = (a_col <= a_row + W) & (a_col >= a_row + 1 + off_ref[0, blk])
        seen = seen & (a_col >= W - (tm * rows + blk * QB))

        def step(i, _):
            for j in range(per):
                at = lanes(i * per + j)
                s = mm(q[blk * QB : (blk + 1) * QB, at], kx[blk * QB : blk * QB + W + QB, at], 1, 1)
                s = jnp.where(seen, s, -jnp.inf)
                top = jnp.max(s, axis=1, keepdims=True)
                e = jnp.exp((s - top) * (1.0 / math.sqrt(dim)))
                whole = jnp.sum(e, axis=1, keepdims=True)
                o = mm(e.astype(BF), vx[blk * QB : blk * QB + W + QB, at])
                put(at, o / whole)
            return 0

        lax.fori_loop(low, high, step, 0)

    def attend_own(low, high):
        for blk in range(1, rows // QB):
            def keep(at, o, blk=blk):
                att[blk * QB : (blk + 1) * QB, at] = o

            attend(blk, keep, low, high)

    def finish(i, _):
        for j in range(per):
            at = lanes(i * per + j)
            cb = cumb[:, at]
            out = inner[:, at] + jnp.exp(cb) * mm(cs_s[...], f_in[:, at])
            mean = jnp.mean(out * out, axis=1, keepdims=True)
            normed = out * lax.rsqrt(mean + 1e-05)
            inner[0:QB, at] = normed[0:QB]
            lo[QB:rows, at] = (normed[QB:rows] + att[QB:rows, at]).astype(BF)
            fall = jnp.exp(cb[rows - 1 : rows, :] - cb)
            ig[:, at] = (gx[:, at] + fall * mm(b_s[...], r_in[:, at])).astype(BF)
        return 0

    def add(at, o):
        lo[0:QB, at] = (inner[0:QB, at] + o).astype(BF)

    start_zscatter(0)

    @pl.when(tm < n_tm - 1)
    def _():
        for halo in halos:
            halo.start()

    attend_own(0, steps // 2)
    late_step(lambda place: place <= 2)
    attend_own(steps // 2, steps)
    lat_t[...] = lat[:, cols].T
    start_zgather(0)
    late_step(lambda place: place > 2)
    start_zscatter(1)
    start_scatter(0)
    lax.fori_loop(0, steps // 2, finish, 0)
    start_zgather(1)
    lax.fori_loop(steps // 2, steps, finish, 0)

    @pl.when(tm > 0)
    def _():
        for halo in halos:
            halo.wait_recv()

    @pl.when(tm == 0)
    def _():
        for buf in (kx, vx):
            buf[0:W, :] = jnp.zeros((W, width), BF)

    start_scatter(1)
    attend(0, add, 0, (steps + 1) // 2)

    own = jnp.where(me < owners, me, 0) if owners < group else me
    owned = pl.ds(pl.multiple_of(own * chunk, chunk), chunk)
    for copies in scatter:
        for _, copy in copies:
            when(me < owners, copy.wait_recv)
    for half in range(2):
        for k in range(1, group):
            other, to = member(k)
            copy = pltpu.make_async_remote_copy(
                src_ref=agf.at[half, owned],
                dst_ref=agf.at[half, owned],
                send_sem=ag_send.at[half, k - 1],
                recv_sem=ag_recv.at[half, k - 1],
                device_id=to, device_id_type=MESH,
            )
            gather[half].append((lax.rem(me + group - k, group) < owners, copy))

        def own_sum(half=half):
            part = term[half, owned, :].astype(F32)
            for k in range(group - 1):
                part = part + rs[half, k].astype(F32)
            agf[half, owned, :] = part.astype(BF)
            for _, copy in gather[half]:
                copy.start()

        when(me < owners, own_sum)

    attend(0, add, (steps + 1) // 2, steps)

    @pl.when(tm < n_tm - 1)
    def _():
        for copy in fwd:
            copy.wait_send()
        for halo in halos:
            halo.wait_send()

    @pl.when(tm > 0)
    def _():
        for copy in rev:
            copy.wait_send()

    for turn in range(2):
        for copy in zscatter[turn] + zgather[turn]:
            copy.wait_send()
        for cond, copy in scatter[turn]:
            when(cond, copy.wait_send)
    for half in range(2):
        for cond, copy in gather[half]:
            when(cond, copy.wait_recv)
    pg_out[...] = agf[...]
    for half in range(2):
        for _, copy in gather[half]:
            when(me < owners, copy.wait_send)


def hand_out(lo_ref, ig_ref, pg_ref, lo_out, ig_out, pg_out, pg, sem):
    copies = [
        pltpu.make_async_copy(src, dst, sem.at[i])
        for i, (src, dst) in enumerate([(lo_ref, lo_out), (ig_ref, ig_out), (pg, pg_out)])
    ]
    copies[0].start()
    copies[1].start()
    states = pg_ref.shape[2]
    for half in range(2):
        pg[:, half * states : (half + 1) * states] = pg_ref[half].astype(F32)
    copies[2].start()
    for copy in copies:
        copy.wait()


def on_device(
    sizes,
    latents,
    proj_input,
    proj_output,
    scan_input,
    log_decay,
    att_queries,
    att_keys,
    att_values,
    scan_cotangent,
    window_offsets,
):
    n_tm, n_z, n_dp = sizes
    clips, rows, model = latents.shape
    assert clips == 1
    width = scan_input.shape[2]
    heads = log_decay.shape[2]
    states = proj_input.shape[1]
    share = model // n_z
    group = n_tm * n_dp
    owners = min(group, share // 16)
    chunk = share // owners
    zrows = rows // n_z
    hbm = pl.BlockSpec(memory_space=pltpu.HBM)
    vmem = pl.BlockSpec(memory_space=pltpu.VMEM)
    smem = pl.BlockSpec(memory_space=pltpu.SMEM)

    def v(shape, kind=BF):
        return pltpu.VMEM(shape, kind)

    dma = pltpu.SemaphoreType.DMA
    layer_out, input_grad, proj_grad = pl.pallas_call(
        functools.partial(kernel, sizes),
        out_shape=(
            v((rows, width)),
            v((rows, width)),
            v((2, share, states)),
        ),
        in_specs=[hbm, hbm, hbm, hbm, vmem, hbm, hbm, hbm, hbm, smem],
        out_specs=(vmem, vmem, vmem),
        scratch_shapes=[
            v((rows, model)), v((model, 2 * states)),
            v((rows, width)), v((rows, width)), v((rows, width)),
            v((W + rows, width)), v((W + rows, width)),
            v((share, rows)),
            v((rows, width), F32), v((heads, rows), F32),
            v((rows, states)), v((rows, states)), v((rows, states)),
            v((rows, rows), F32), v((rows, rows), F32),
            v((rows, width)), v((rows, width)),
            v((rows, width), F32), v((rows, width), F32), v((rows, width), F32),
            v((states, width), F32), v((states, width)), v((states, width)),
            v((states, width), F32), v((states, width)), v((states, width)),
            v((2, rows, states)), v((2, n_z - 1, zrows, states)), v((2, rows, states)),
            v((2, share, states)), v((2, group - 1, chunk, states)), v((2, share, states)),
            dma((8,)), dma((2, 2)), dma((2, 2)), dma((2,)), dma((2,)),
            dma((2, n_z - 1)), dma((2, n_z - 1)), dma((2, n_z - 1)), dma((2, n_z - 1)),
            dma((2, group - 1)), dma((2, group - 1)), dma((2, group - 1)), dma((2, group - 1)),
        ],
        compiler_params=pltpu.CompilerParams(
            collective_id=0, has_side_effects=True, vmem_limit_bytes=60 * 1024 * 1024
        ),
    )(
        latents[0], proj_input, proj_output, scan_input[0], log_decay[0].T,
        att_queries[0], att_keys[0], att_values[0], scan_cotangent[0], window_offsets,
    )
    layer_out, input_grad, proj_grad = pl.pallas_call(
        hand_out,
        out_shape=(
            jax.ShapeDtypeStruct((rows, width), BF),
            jax.ShapeDtypeStruct((rows, width), BF),
            jax.ShapeDtypeStruct((share, 2 * states), F32),
        ),
        in_specs=[vmem, vmem, vmem],
        out_specs=(hbm, hbm, hbm),
        scratch_shapes=[v((share, 2 * states), F32), dma((3,))],
        compiler_params=pltpu.CompilerParams(vmem_limit_bytes=8 * 1024 * 1024),
    )(layer_out, input_grad, proj_grad)
    return layer_out[None], input_grad[None], proj_grad


def solution(mesh):
    sizes = (mesh.shape["tm"], mesh.shape["space"], mesh.shape["dp"])
    return jax.shard_map(
        functools.partial(on_device, sizes),
        mesh=mesh,
        in_specs=(
            P("dp", "tm", None),
            P(),
            P(),
            P("dp", "tm", "space"),
            P("dp", "tm", "space"),
            P("dp", "tm", "space"),
            P("dp", "tm", "space"),
            P("dp", "tm", "space"),
            P("dp", "tm", "space"),
            P("dp", "tm"),
        ),
        out_specs=(P("dp", "tm", "space"), P("dp", "tm", "space"), P("space", None)),
        check_vma=False,
    )
```

```python
import functools
import math

import jax
import jax.numpy as jnp
from jax import lax
from jax.experimental import pallas as pl
from jax.experimental.pallas import tpu as pltpu
from jax.sharding import PartitionSpec as P

W = 128
QB = 128
MESH = pl.DeviceIdType.MESH
BF = jnp.bfloat16
F32 = jnp.float32


def mm(a, b, ca=1, cb=0):
    return lax.dot_general(a, b, (((ca,), (cb,)), ((), ())), preferred_element_type=F32)


def three(a):
    first = a.astype(BF).astype(F32)
    second = (a - first).astype(BF).astype(F32)
    return jnp.concatenate([first, second, a - first - second], axis=0).astype(BF)


def kernel(
    sizes,
    lat_h, pi_h, po_h, x_h, ld_ref, q_h, k_h, v_h, g_h, off_ref,
    lo, ig, pg_out,
    lat, proj, x, g, q, kx, vx, lat_t,
    cumb, cumt, b_s, c_s, cs_s, kern, wsum, xw, rg, inner, gx, att,
    f_fresh, f_in, f_out, r_fresh, r_in, r_out,
    base, both, rz, zfull, term, rs, agf,
    load_sem, chain_send, chain_recv, halo_send, halo_recv,
    zs_send, zs_recv, zg_send, zg_recv, rs_send, rs_recv, ag_send, ag_recv,
):
    n_tm, n_z, n_dp = sizes
    rows, width = x.shape
    heads = ld_ref.shape[0]
    dim = width // heads
    states = proj.shape[1] // 2
    scale = 1.0 / math.sqrt(states)
    group = n_tm * n_dp
    share = lat.shape[1] // n_z
    owners = min(group, share // 16)
    chunk = share // owners
    zrows = rows // n_z
    tm = lax.axis_index("tm")
    z = lax.axis_index("space")
    dp = lax.axis_index("dp")
    me = dp * n_tm + tm

    def member(k):
        other = lax.rem(me + k, group)
        return other, {"dp": other // n_tm, "tm": lax.rem(other, n_tm)}

    def zmember(k):
        other = lax.rem(z + k, n_z)
        return other, {"space": other}

    loads = [
        pltpu.make_async_copy(src, dst, load_sem.at[i])
        for i, (src, dst) in enumerate(
            [
                (lat_h, lat), (pi_h, proj.at[:, 0:states]),
                (po_h, proj.at[:, states : 2 * states]), (x_h, x), (g_h, g),
                (k_h, kx.at[pl.ds(W, rows)]), (v_h, vx.at[pl.ds(W, rows)]), (q_h, q),
            ]
        )
    ]
    for load in loads[3:5] + loads[:3]:
        load.start()

    barrier = pltpu.get_barrier_semaphore()
    for k in range(1, group):
        pl.semaphore_signal(barrier, inc=1, device_id=member(k)[1], device_id_type=MESH)
    for k in range(1, n_z):
        pl.semaphore_signal(barrier, inc=1, device_id=zmember(k)[1], device_id_type=MESH)

    row_i = lax.broadcasted_iota(jnp.int32, (rows, rows), 0)
    col_i = lax.broadcasted_iota(jnp.int32, (rows, rows), 1)
    upper = (row_i <= col_i).astype(BF)
    sums = mm(three(ld_ref[...]), upper)
    cum = sums[:heads] + sums[heads : 2 * heads] + sums[2 * heads :]
    cumt[...] = cum
    spread = (
        lax.broadcasted_iota(jnp.int32, (3 * heads, width), 1) // dim
        == lax.rem(lax.broadcasted_iota(jnp.int32, (3 * heads, width), 0), heads)
    ).astype(BF)
    cumb[...] = mm(three(cum), spread, 0, 0)

    for load in loads[3:5]:
        load.wait()
    for load in loads[5:]:
        load.start()
    total = cumb[rows - 1 : rows, :]
    rg[...] = (jnp.exp(cumb[...]) * g[...].astype(F32)).astype(BF)
    xw[...] = (jnp.exp(total - cumb[...]) * x[...].astype(F32)).astype(BF)
    for load in loads[:3]:
        load.wait()
    bc = mm(lat[...], proj[...]).astype(BF)
    b_s[...] = bc[:, :states]
    c_s[...] = bc[:, states:]
    cs_s[...] = (bc[:, states:].astype(F32) * scale).astype(BF)
    f_fresh[...] = mm(b_s[...], xw[...], 0, 0)
    r_fresh[...] = mm(cs_s[...], rg[...], 0, 0)
    pl.semaphore_wait(barrier, group - 1 + n_z - 1)

    up = lax.rem(tm + 1, n_tm)
    down = lax.rem(tm + n_tm - 1, n_tm)
    pieces = [pl.ds(0, width // 2), pl.ds(width // 2, width // 2)]

    def chain(i, src, dst, to):
        return [
            pltpu.make_async_remote_copy(
                src_ref=src.at[:, at], dst_ref=dst.at[:, at],
                send_sem=chain_send.at[i, p], recv_sem=chain_recv.at[i, p],
                device_id={"tm": to}, device_id_type=MESH,
            )
            for p, at in enumerate(pieces)
        ]

    fwd = chain(0, f_out, f_in, up)
    rev = chain(1, r_out, r_in, down)

    def chain_step(copies, place, fresh, src, dst):
        @pl.when(place == 0)
        def _():
            dst[...] = jnp.zeros_like(dst)

        for copy, at in zip(copies, pieces):
            @pl.when(place > 0)
            def _(copy=copy):
                copy.wait_recv()

            @pl.when(place < n_tm - 1)
            def _(copy=copy, at=at):
                carried = jnp.exp(cumb[rows - 1 : rows, at])
                src[:, at] = (carried * dst[:, at].astype(F32) + fresh[:, at]).astype(BF)
                copy.start()

    rplace = n_tm - 1 - tm
    early_fwd = 2 * tm < n_tm
    half_of = [jnp.where(early_fwd, 1, 0), jnp.where(early_fwd, 0, 1)]

    def early_step(ready):
        @pl.when(early_fwd & ready(tm))
        def _():
            chain_step(fwd, tm, f_fresh, f_out, f_in)

        @pl.when(jnp.logical_not(early_fwd) & ready(rplace))
        def _():
            chain_step(rev, rplace, r_fresh, r_out, r_in)

    def late_step(ready):
        @pl.when(early_fwd & ready(rplace))
        def _():
            chain_step(rev, rplace, r_fresh, r_out, r_in)

        @pl.when(jnp.logical_not(early_fwd) & ready(tm))
        def _():
            chain_step(fwd, tm, f_fresh, f_out, f_in)

    halos = [
        pltpu.make_async_remote_copy(
            src_ref=buf.at[pl.ds(rows, W)], dst_ref=buf.at[pl.ds(0, W)],
            send_sem=halo_send.at[i], recv_sem=halo_recv.at[i],
            device_id={"tm": up}, device_id_type=MESH,
        )
        for i, buf in enumerate((kx, vx))
    ]
    per = 4 if heads % 4 == 0 else heads
    steps = heads // per
    pair = 2 if heads % 2 == 0 else 1
    turns = heads // pair
    early_step(lambda place: place == 0)
    kern[...] = mm(cs_s[...], b_s[...], 1, 1)
    wsum[...] = jnp.zeros_like(wsum)
    for load in loads[5:]:
        load.wait()

    assert rows == 2 * dim
    tri = lax.broadcasted_iota(jnp.int32, (dim, dim), 0) >= lax.broadcasted_iota(
        jnp.int32, (dim, dim), 1
    )

    def lanes(h):
        return pl.ds(pl.multiple_of(h * dim, dim), dim)

    def local_step(i, _):
        early_step(lambda place: (place == i) & (i > 0))

        w00, w10, w11 = wsum[:dim, :dim], wsum[dim:, :dim], wsum[dim:, dim:]
        for j in range(pair):
            h = i * pair + j
            at = lanes(h)
            ct = cumt[pl.ds(h, 1), :]
            cb0, cb1 = cumb[:dim, at], cumb[dim:, at]
            d00 = jnp.exp(jnp.where(tri, cb0 - ct[:, :dim], -jnp.inf))
            d10 = jnp.exp(cb1 - ct[:, :dim])
            d11 = jnp.exp(jnp.where(tri, cb1 - ct[:, dim:], -jnp.inf))
            m00 = (kern[:dim, :dim] * d00).astype(BF)
            m10 = (kern[dim:, :dim] * d10).astype(BF)
            m11 = (kern[dim:, dim:] * d11).astype(BF)
            xh, gh = x[:, at], g[:, at]
            p00 = mm(gh[:dim], xh[:dim], 1, 1)
            p1 = mm(gh[dim:], xh, 1, 1)
            w00 = w00 + p00 * d00
            w10 = w10 + p1[:, :dim] * d10
            w11 = w11 + p1[:, dim:] * d11
            inner[:dim, at] = mm(m00, xh[:dim])
            inner[dim:, at] = mm(jnp.concatenate([m10, m11], axis=1), xh)
            gx[:dim, at] = mm(jnp.concatenate([m00, m10], axis=0), gh, 0, 0)
            gx[dim:, at] = mm(m11, gh[dim:], 0, 0)
        wsum[:dim, :dim] = w00
        wsum[dim:, :dim] = w10
        wsum[dim:, dim:] = w11
        return 0

    lax.fori_loop(0, turns, local_step, 0)

    early_step(lambda place: place >= turns)

    weigh = (wsum[...] * scale).astype(BF)
    base[1] = mm(weigh, b_s[...])
    base[0] = mm(weigh, c_s[...], 0, 0)
    zscatter, zgather, scatter, gather = [[], []], [[], []], [[], []], [[], []]
    mine = pl.ds(pl.multiple_of(z * zrows, zrows), zrows)
    cols = pl.ds(pl.multiple_of(z * share, share), share)

    def fill_c():
        both[1] = (base[1] + mm(rg[...], f_in[...], 1, 1) * scale).astype(BF)

    def fill_b():
        both[0] = (base[0] + mm(xw[...], r_in[...], 1, 1)).astype(BF)

    def start_zscatter(turn):
        c_now = early_fwd if turn == 0 else jnp.logical_not(early_fwd)
        pl.when(c_now)(fill_c)
        pl.when(jnp.logical_not(c_now))(fill_b)
        half = half_of[turn]
        for k in range(1, n_z):
            other, to = zmember(k)
            copy = pltpu.make_async_remote_copy(
                src_ref=both.at[half, pl.ds(pl.multiple_of(other * zrows, zrows), zrows)],
                dst_ref=rz.at[half, k - 1],
                send_sem=zs_send.at[half, k - 1],
                recv_sem=zs_recv.at[half, k - 1],
                device_id=to, device_id_type=MESH,
            )
            zscatter[turn].append(copy)
            copy.start()

    def start_zgather(turn):
        half = half_of[turn]
        for copy in zscatter[turn]:
            copy.wait_recv()
        part = both[half, mine, :].astype(F32)
        for k in range(n_z - 1):
            part = part + rz[half, k].astype(F32)
        zfull[half, mine, :] = part.astype(BF)
        for k in range(1, n_z):
            other, to = zmember(k)
            copy = pltpu.make_async_remote_copy(
                src_ref=zfull.at[half, mine],
                dst_ref=zfull.at[half, mine],
                send_sem=zg_send.at[half, k - 1],
                recv_sem=zg_recv.at[half, k - 1],
                device_id=to, device_id_type=MESH,
            )
            zgather[turn].append(copy)
            copy.start()

    def when(cond, action):
        if owners == group:
            action()
        else:
            pl.when(cond)(action)

    def start_scatter(turn):
        half = half_of[turn]
        for copy in zgather[turn]:
            copy.wait_recv()
        grad = mm(lat_t[...], zfull[half])
        term[half] = (grad * (1.0 / math.sqrt(n_dp * rows * n_tm))).astype(BF)
        for k in range(1, group):
            other, to = member(k)
            at = jnp.where(other < owners, other, 0) if owners < group else other
            copy = pltpu.make_async_remote_copy(
                src_ref=term.at[half, pl.ds(pl.multiple_of(at * chunk, chunk), chunk)],
                dst_ref=rs.at[half, k - 1],
                send_sem=rs_send.at[half, k - 1],
                recv_sem=rs_recv.at[half, k - 1],
                device_id=to, device_id_type=MESH,
            )
            scatter[turn].append((other < owners, copy))
            when(other < owners, copy.start)

    a_row = lax.broadcasted_iota(jnp.int32, (QB, W + QB), 0)
    a_col = lax.broadcasted_iota(jnp.int32, (QB, W + QB), 1)

    def attend(blk, put, low, high):
        seen = (a_col <= a_row + W) & (a_col >= a_row + 1 + off_ref[0, blk])
        seen = seen & (a_col >= W - (tm * rows + blk * QB))

        def step(i, _):
            for j in range(per):
                at = lanes(i * per + j)
                s = mm(q[blk * QB : (blk + 1) * QB, at], kx[blk * QB : blk * QB + W + QB, at], 1, 1)
                s = jnp.where(seen, s, -jnp.inf)
                top = jnp.max(s, axis=1, keepdims=True)
                e = jnp.exp((s - top) * (1.0 / math.sqrt(dim)))
                whole = jnp.sum(e, axis=1, keepdims=True)
                o = mm(e.astype(BF), vx[blk * QB : blk * QB + W + QB, at])
                put(at, o / whole)
            return 0

        lax.fori_loop(low, high, step, 0)

    def attend_own(low, high):
        for blk in range(1, rows // QB):
            def keep(at, o, blk=blk):
                att[blk * QB : (blk + 1) * QB, at] = o

            attend(blk, keep, low, high)

    def finish(i, _):
        for j in range(per):
            at = lanes(i * per + j)
            cb = cumb[:, at]
            out = inner[:, at] + jnp.exp(cb) * mm(cs_s[...], f_in[:, at])
            mean = jnp.mean(out * out, axis=1, keepdims=True)
            normed = out * lax.rsqrt(mean + 1e-05)
            inner[0:QB, at] = normed[0:QB]
            lo[QB:rows, at] = (normed[QB:rows] + att[QB:rows, at]).astype(BF)
            fall = jnp.exp(cb[rows - 1 : rows, :] - cb)
            ig[:, at] = (gx[:, at] + fall * mm(b_s[...], r_in[:, at])).astype(BF)
        return 0

    def add(at, o):
        lo[0:QB, at] = (inner[0:QB, at] + o).astype(BF)

    start_zscatter(0)

    @pl.when(tm < n_tm - 1)
    def _():
        for halo in halos:
            halo.start()

    attend_own(0, steps // 2)
    late_step(lambda place: place <= 2)
    attend_own(steps // 2, steps)
    lat_t[...] = lat[:, cols].T
    start_zgather(0)
    late_step(lambda place: place > 2)
    start_zscatter(1)
    start_scatter(0)
    lax.fori_loop(0, steps // 2, finish, 0)
    start_zgather(1)
    lax.fori_loop(steps // 2, steps, finish, 0)

    @pl.when(tm > 0)
    def _():
        for halo in halos:
            halo.wait_recv()

    @pl.when(tm == 0)
    def _():
        for buf in (kx, vx):
            buf[0:W, :] = jnp.zeros((W, width), BF)

    start_scatter(1)
    attend(0, add, 0, (steps + 1) // 2)

    own = jnp.where(me < owners, me, 0) if owners < group else me
    owned = pl.ds(pl.multiple_of(own * chunk, chunk), chunk)
    for copies in scatter:
        for _, copy in copies:
            when(me < owners, copy.wait_recv)
    for half in range(2):
        for k in range(1, group):
            other, to = member(k)
            copy = pltpu.make_async_remote_copy(
                src_ref=agf.at[half, owned],
                dst_ref=agf.at[half, owned],
                send_sem=ag_send.at[half, k - 1],
                recv_sem=ag_recv.at[half, k - 1],
                device_id=to, device_id_type=MESH,
            )
            gather[half].append((lax.rem(me + group - k, group) < owners, copy))

        def own_sum(half=half):
            part = term[half, owned, :].astype(F32)
            for k in range(group - 1):
                part = part + rs[half, k].astype(F32)
            agf[half, owned, :] = part.astype(BF)
            for _, copy in gather[half]:
                copy.start()

        when(me < owners, own_sum)

    attend(0, add, (steps + 1) // 2, steps)

    @pl.when(tm < n_tm - 1)
    def _():
        for copy in fwd:
            copy.wait_send()
        for halo in halos:
            halo.wait_send()

    @pl.when(tm > 0)
    def _():
        for copy in rev:
            copy.wait_send()

    for turn in range(2):
        for copy in zscatter[turn] + zgather[turn]:
            copy.wait_send()
        for cond, copy in scatter[turn]:
            when(cond, copy.wait_send)
    for half in range(2):
        for cond, copy in gather[half]:
            when(cond, copy.wait_recv)
    pg_out[...] = agf[...]
    for half in range(2):
        for _, copy in gather[half]:
            when(me < owners, copy.wait_send)


def hand_out(lo_ref, ig_ref, pg_ref, lo_out, ig_out, pg_out, pg, sem):
    copies = [
        pltpu.make_async_copy(src, dst, sem.at[i])
        for i, (src, dst) in enumerate([(lo_ref, lo_out), (ig_ref, ig_out), (pg, pg_out)])
    ]
    copies[0].start()
    copies[1].start()
    states = pg_ref.shape[2]
    for half in range(2):
        pg[:, half * states : (half + 1) * states] = pg_ref[half].astype(F32)
    copies[2].start()
    for copy in copies:
        copy.wait()


def on_device(
    sizes,
    latents,
    proj_input,
    proj_output,
    scan_input,
    log_decay,
    att_queries,
    att_keys,
    att_values,
    scan_cotangent,
    window_offsets,
):
    n_tm, n_z, n_dp = sizes
    clips, rows, model = latents.shape
    assert clips == 1
    width = scan_input.shape[2]
    heads = log_decay.shape[2]
    states = proj_input.shape[1]
    share = model // n_z
    group = n_tm * n_dp
    owners = min(group, share // 16)
    chunk = share // owners
    zrows = rows // n_z
    hbm = pl.BlockSpec(memory_space=pltpu.HBM)
    vmem = pl.BlockSpec(memory_space=pltpu.VMEM)
    smem = pl.BlockSpec(memory_space=pltpu.SMEM)

    def v(shape, kind=BF):
        return pltpu.VMEM(shape, kind)

    dma = pltpu.SemaphoreType.DMA
    layer_out, input_grad, proj_grad = pl.pallas_call(
        functools.partial(kernel, sizes),
        out_shape=(
            v((rows, width)),
            v((rows, width)),
            v((2, share, states)),
        ),
        in_specs=[hbm, hbm, hbm, hbm, vmem, hbm, hbm, hbm, hbm, smem],
        out_specs=(vmem, vmem, vmem),
        scratch_shapes=[
            v((rows, model)), v((model, 2 * states)),
            v((rows, width)), v((rows, width)), v((rows, width)),
            v((W + rows, width)), v((W + rows, width)),
            v((share, rows)),
            v((rows, width), F32), v((heads, rows), F32),
            v((rows, states)), v((rows, states)), v((rows, states)),
            v((rows, rows), F32), v((rows, rows), F32),
            v((rows, width)), v((rows, width)),
            v((rows, width), F32), v((rows, width), F32), v((rows, width), F32),
            v((states, width), F32), v((states, width)), v((states, width)),
            v((states, width), F32), v((states, width)), v((states, width)),
            v((2, rows, states), F32), v((2, rows, states)), v((2, n_z - 1, zrows, states)), v((2, rows, states)),
            v((2, share, states)), v((2, group - 1, chunk, states)), v((2, share, states)),
            dma((8,)), dma((2, 2)), dma((2, 2)), dma((2,)), dma((2,)),
            dma((2, n_z - 1)), dma((2, n_z - 1)), dma((2, n_z - 1)), dma((2, n_z - 1)),
            dma((2, group - 1)), dma((2, group - 1)), dma((2, group - 1)), dma((2, group - 1)),
        ],
        compiler_params=pltpu.CompilerParams(
            collective_id=0, has_side_effects=True, vmem_limit_bytes=60 * 1024 * 1024
        ),
    )(
        latents[0], proj_input, proj_output, scan_input[0], log_decay[0].T,
        att_queries[0], att_keys[0], att_values[0], scan_cotangent[0], window_offsets,
    )
    layer_out, input_grad, proj_grad = pl.pallas_call(
        hand_out,
        out_shape=(
            jax.ShapeDtypeStruct((rows, width), BF),
            jax.ShapeDtypeStruct((rows, width), BF),
            jax.ShapeDtypeStruct((share, 2 * states), F32),
        ),
        in_specs=[vmem, vmem, vmem],
        out_specs=(hbm, hbm, hbm),
        scratch_shapes=[v((share, 2 * states), F32), dma((3,))],
        compiler_params=pltpu.CompilerParams(vmem_limit_bytes=8 * 1024 * 1024),
    )(layer_out, input_grad, proj_grad)
    return layer_out[None], input_grad[None], proj_grad


def solution(mesh):
    sizes = (mesh.shape["tm"], mesh.shape["space"], mesh.shape["dp"])
    return jax.shard_map(
        functools.partial(on_device, sizes),
        mesh=mesh,
        in_specs=(
            P("dp", "tm", None),
            P(),
            P(),
            P("dp", "tm", "space"),
            P("dp", "tm", "space"),
            P("dp", "tm", "space"),
            P("dp", "tm", "space"),
            P("dp", "tm", "space"),
            P("dp", "tm", "space"),
            P("dp", "tm"),
        ),
        out_specs=(P("dp", "tm", "space"), P("dp", "tm", "space"), P("space", None)),
        check_vma=False,
    )
```
